512 devices in a mesh: rows: 32 (over x, z_lo), chol: 16 (over z_hi, y, core).
Axes of the slice: x: 4, y: 4, z: 16 (z_hi: 2, z_lo: 8; z = z_hi * 8 + z_lo), core: 2. Of those that a mesh axis runs over, the one named last changes fastest.
Arguments:
- walkers: float32 [16, 1024, 128], P(None, 'rows'), may hold values from -9 to 9
- trial: float32 [1024, 128], replicated, may hold values from -0.2 to 0.2
- cholesky: float32 [256, 1048576], P('chol', 'rows'), may hold values from -0.25 to 0.25
- noise: float32 [16, 256], P(None, 'chol'), may hold values from -4 to 4
Outputs:
- propagated: float32 [16, 1024, 128], P('chol', 'rows')
- log_weight: float32 [16], replicated
The draws below stay inside these ranges and needn't reach their ends.
All inputs are finite; a program needn't handle non-finite values.
Results may differ from the reference program's by a relative error of at most 0.00019.
Values sent between devices are 32-bit elements; how exact they have to be, the bound alone decides.
A program may use at most 64 MiB of HBM per device.

```python
import jax
import jax.numpy as jnp
from jax import lax

M = 1024
NE = 128
TAYLOR = 6
NCHOL = 256
W = 16


def shared_base(key):
    return jnp.clip(jax.random.normal(key, (M, NE), jnp.float32), -6.0, 6.0)


def draw_trial(key, part):
    base = shared_base(key)
    return base / jnp.sqrt(jnp.float32(M))


def draw_walkers(key, part):
    base = shared_base(key)
    key = jax.random.fold_in(key, 11)
    spread = jnp.clip(jax.random.normal(key, (W, M, NE), jnp.float32), -5.0, 5.0)
    return base[None, :, :] + 0.5 * spread


def draw_cholesky(key, part):
    key = jax.random.fold_in(key, 23)
    first, second = jax.random.split(key)
    values = jnp.clip(jax.random.normal(first, (NCHOL, M * M), jnp.float32), -6.0, 6.0)
    values = values * (16.0 / jnp.sqrt(jnp.float32(NCHOL * M)))
    index = jnp.arange(M * M, dtype=jnp.int32)
    diagonal = (index // M == index % M).astype(jnp.float32)
    weights = jax.random.uniform(second, (NCHOL, 1), jnp.float32, -1.0, 1.0) * (5.0 / NE)
    return values + diagonal[None, :] * weights


def steps_of(stream_key, extent, cuts, smallest, largest):
    def one(axis_at, shards_of):
        steps = jax.random.uniform(jax.random.fold_in(jax.random.fold_in(stream_key, 6), axis_at), (shards_of,), jnp.float32, smallest / len(cuts), largest / len(cuts))
        return jnp.repeat(jnp.exp(steps), extent[axis_at] // shards_of).reshape((-1,) + (1,) * (len(extent) - axis_at - 1))

    level = one(*cuts[0])
    for cut in cuts[1:]:
        level = level * one(*cut)
    return level


def scatter_about(key, dims, width, bound, cuts=(), kind=jnp.bfloat16):
    entries = jax.random.normal(key, dims, jnp.float32) * width
    if len(cuts) > 0:
        entries = steps_of(key, dims, cuts, -0.22, 0.18) * entries
    return jnp.clip(entries, min=-bound, max=bound).astype(kind)


def setup_inputs(seed: int = 0) -> dict:
    key_list = jax.random.split(jax.random.key(seed), 5)
    return {
        "walkers": draw_walkers(jax.random.fold_in(key_list[4], 71), 0),
        "trial": draw_trial(jax.random.fold_in(key_list[4], 71), 0),
        "cholesky": draw_cholesky(jax.random.fold_in(key_list[4], 71), 0),
        "noise": scatter_about(key_list[3], (W, NCHOL), 1.0, 4.0, ((1, 16),), jnp.float32),
    }


def factor_solve(factor, right):
    middle = lax.linalg.triangular_solve(factor, right, left_side=True, lower=True, transpose_a=False)
    return lax.linalg.triangular_solve(factor, middle, left_side=True, lower=True, transpose_a=True)

def reference(walkers, trial, cholesky, noise):
    high = lax.Precision.HIGHEST
    correlation = jnp.einsum('ia,wib->wab', trial, walkers, precision=high)
    gram = jnp.einsum('wab,wac->wbc', correlation, correlation, precision=high)
    factor = jnp.linalg.cholesky(gram)
    right = jnp.einsum('wab,ka->wbk', correlation, trial, precision=high)
    inverse_trial = factor_solve(factor, right)
    green = jnp.einsum('wia,wak->wik', walkers, inverse_trial, precision=high)
    green = green.reshape(green.shape[0], M * M)
    bias = 0.1 * lax.dot_general(green.astype(jnp.float32), cholesky.astype(jnp.float32), (((1,), (1,)), ((), ())), precision=high, preferred_element_type=jnp.float32)
    field = noise - bias
    log_weight = jnp.sum(field * bias - 0.5 * bias * bias, axis=1)
    potential = 0.1 * jnp.dot(field.astype(jnp.float32), cholesky.astype(jnp.float32), precision=high, preferred_element_type=jnp.float32)
    potential = potential.reshape(potential.shape[0], M, M)
    term = walkers
    total = walkers
    for order in range(1, TAYLOR + 1):
        term = jnp.einsum('wik,wka->wia', potential, term, precision=high) / float(order)
        total = total + term
    return (total, log_weight)
```

```python
import functools

import jax
import jax.numpy as jnp
from jax import lax
from jax.experimental import pallas as pl
from jax.experimental.pallas import tpu as pltpu
from jax.sharding import PartitionSpec as P

M = 1024
NE = 128
TAYLOR = 6
NX, NZ, NH, NY, NK = 4, 8, 2, 4, 2
ROWS = NX * NZ
YK = NY * NK
BLOCK = M // ROWS
W = 16
OWN = 16
F32 = jnp.float32
BF16 = jnp.bfloat16
MESH_ID = pl.DeviceIdType.MESH
NT = (((1,), (1,)), ((), ()))
NN = (((1,), (0,)), ((), ()))
TN = (((0,), (0,)), ((), ()))


def exact(a, b, dims):
    return lax.dot_general(a, b, dims, precision=lax.Precision.HIGHEST, preferred_element_type=F32)


def split(a):
    top = a.astype(BF16)
    return top, (a - top.astype(F32)).astype(BF16)


def dot3(a, b, dims):
    def one(p, q):
        return lax.dot_general(p, q, dims, preferred_element_type=F32)

    return one(a[0], b[0]) + (one(a[0], b[1]) + one(a[1], b[0]))


def sub(index):
    return lax.broadcasted_iota(jnp.int32, index, 0)


def lane(index):
    return lax.broadcasted_iota(jnp.int32, index, 1)


def eliminate(mats):
    row8 = sub((8, NE))
    out = []
    for mat in mats:
        spread = [jnp.broadcast_to(mat[:, u : u + 1], (NE, NE)) for u in range(8)]
        small = [s[0:8] for s in spread]
        top = jnp.where(lane((8, NE)) < 8, (lane((8, NE)) == row8).astype(F32), mat[0:8])
        for t in range(8):
            inverse = 1.0 / jnp.broadcast_to(small[t][t : t + 1], (8, NE))
            pivot = small[t]
            for u in range(t + 1, 8):
                scaled = jnp.broadcast_to(small[u][t : t + 1], (8, NE)) * inverse
                small[u] = jnp.where(row8 == t, scaled, small[u] - pivot * scaled)
            scaled = jnp.broadcast_to(top[t : t + 1], (8, NE)) * inverse
            top = jnp.where(row8 == t, scaled, top - pivot * scaled)
        rest = jnp.where(lane((NE - 8, NE)) < 8, 0.0, mat[8:])
        for u in range(8):
            rest = rest - spread[u][8:] * top[u : u + 1]
        out.append(pltpu.roll(jnp.concatenate([rest, top], axis=0), NE - 8, 1))
    return tuple(out)


def kernel(
    walkers, trial, cholesky, noise, out, weight,
    slab, slab_top, slab_low, lt, cpart, crs, cag, wx, tbuf, vall, brs, pot, rc, ry, rz, px, fx, turn, lws, lwz,
    sem_l, s_c, r_c, s_a, r_a, s_w, r_w, s_t, r_t, s_v, r_v, s_b, r_b, s_k, r_k, s_y, r_y, s_z, r_z, s_p, r_p, s_f, r_f, s_l, r_l, s_m, r_m,
):
    r = lax.axis_index("rows")
    c = lax.axis_index("chol")
    x, z = r // NZ, r % NZ
    h, yk = c // YK, c % YK
    y, k = yk // NK, yk % NK

    def at(row, col):
        return (row, col)

    def row_peer(j):
        return at((r + j) % ROWS, c)

    def x_peer(j):
        return at(((x + j) % NX) * NZ + z, c)

    def z_peer(j):
        return at(x * NZ + (z + j) % NZ, c)

    def yk_peer(j):
        return at(r, h * YK + (yk + j) % YK)

    def y_peer(j):
        return at(r, h * YK + ((y + j) % NY) * NK + k)

    core_peer = at(r, h * YK + y * NK + (1 - k))
    h_peer = at(r, (1 - h) * YK + yk)

    def send(src, dst, ss, rs, dev):
        return pltpu.make_async_remote_copy(
            src_ref=src, dst_ref=dst, send_sem=ss, recv_sem=rs, device_id=dev, device_id_type=MESH_ID
        )

    def each(n, step):
        def run(j, carry):
            step(j)
            return carry

        lax.fori_loop(1, n, run, 0)

    def load(i):
        return pltpu.make_async_copy(
            cholesky.at[:, pl.ds(pl.multiple_of(i * M, M), M)], slab.at[pl.ds(pl.multiple_of(i * OWN, OWN), OWN)], sem_l.at[i]
        )

    def load_start(i, carry):
        load(i).start()
        return carry

    def load_wait(i, carry):
        load(i).wait()
        return carry

    lax.fori_loop(0, BLOCK, load_start, 0)

    barrier = pltpu.get_barrier_semaphore()

    def greet(dev):
        pl.semaphore_signal(barrier, inc=1, device_id=dev, device_id_type=MESH_ID)

    each(ROWS, lambda j: greet(row_peer(j)))
    each(YK, lambda j: greet(yk_peer(j)))
    greet(h_peer)

    own_trial = trial[pl.ds(pl.multiple_of(r * BLOCK, BLOCK), BLOCK), :]
    for s in range(NH):
        cpart[s * NE : (s + 1) * NE, :] = exact(own_trial, walkers[s * YK + yk], TN)
    wx[x] = walkers[c]

    pl.semaphore_wait(barrier, ROWS - 1 + YK - 1 + 1)

    def c_copy(j):
        part = pl.ds(pl.multiple_of(8 * ((r + j) % ROWS), 8), 8)
        return send(cpart.at[part], crs.at[j], s_c.at[j], r_c.at[j], row_peer(j))

    each(ROWS, lambda j: c_copy(j).start())

    def w_copy(j):
        return send(wx.at[x], wx.at[x], s_w.at[j], r_w.at[j], x_peer(j))

    each(NX, lambda j: w_copy(j).start())

    lax.fori_loop(0, BLOCK, load_wait, 0)
    trial_split = split(trial[...])

    def prepare(b, carry):
        rows = pl.ds(pl.multiple_of(b * 128, 128), 128)
        block = slab[rows, :]
        top, low = split(block)
        lt[rows, :] = dot3((top, low), trial_split, NN)
        for t in range(NZ):
            at_tile, at_lane = t // 4, (t % 4) * BLOCK
            pieces = [
                block[:, (2 * q + at_tile) * 128 + at_lane : (2 * q + at_tile) * 128 + at_lane + BLOCK] for q in range(NX)
            ]
            top, low = split(jnp.concatenate(pieces, axis=1))
            slab_top[rows, t * 128 : (t + 1) * 128] = top
            slab_low[rows, t * 128 : (t + 1) * 128] = low
        return carry

    lax.fori_loop(0, 4, prepare, 0)

    crs[0] = cpart[pl.ds(pl.multiple_of(8 * r, 8), 8), :]
    each(ROWS, lambda j: c_copy(j).wait_recv())
    cag[r] = jnp.sum(crs[...], axis=0)

    def a_copy(j):
        return send(cag.at[r], cag.at[r], s_a.at[j], r_a.at[j], row_peer(j))

    each(ROWS, lambda j: a_copy(j).start())

    each(NX, lambda j: w_copy(j).wait_recv())
    turn[...] = jnp.transpose(wx[...].reshape(NE, NE))
    first = turn[pl.ds(pl.multiple_of(x * BLOCK, BLOCK), BLOCK), :]
    tbuf[0, z] = first

    def t_copy(n, j):
        return send(tbuf.at[n, z], tbuf.at[n, z], s_t.at[n, j], r_t.at[n, j], z_peer(j))

    each(NZ, lambda j: t_copy(0, j).start())

    each(ROWS, lambda j: a_copy(j).wait_recv())
    both = cag[...].reshape(NH * NE, NE)
    corr = [both[s * NE : (s + 1) * NE] for s in range(NH)]
    grams = tuple(exact(m, m, TN) for m in corr)
    inverses = lax.fori_loop(0, NE // 8, lambda i, m: eliminate(m), grams)
    for s in range(NH):
        left = exact(walkers[s * YK + yk], inverses[s], NN)
        vall[yk, s] = exact(left, corr[s], NT)

    def v_copy(j):
        return send(vall.at[yk], vall.at[yk], s_v.at[j], r_v.at[j], yk_peer(j))

    each(YK, lambda j: v_copy(j).start())

    full_sub, full_lane = sub((128, 128)), lane((128, 128))
    pick_w = (sub((128, W)) // 8 == lane((128, W))).astype(F32)
    pick_g = (lane((OWN, 128)) % OWN == sub((OWN, 128))).astype(F32)
    noise_wide = exact(exact(pick_w, noise[...], NN), pick_g, NN)
    noise8 = jnp.zeros((8, 128), F32)
    for s in range(2):
        pick = (lane((8, OWN)) == sub((8, OWN)) + 8 * s).astype(F32)
        place = (lane((W, 128)) == sub((W, 128)) + W * s).astype(F32)
        noise8 = noise8 + exact(exact(pick, noise[...], NT), place, NN)
    rows512, lanes512 = sub((2 * 512, 128)), lane((2 * 512, 128))
    walker_of = ((rows512 // BLOCK) % NH) * YK + (rows512 // (BLOCK * NH)) % YK
    collect = (lanes512 == (rows512 // 512) * W + walker_of).astype(F32)
    lt_split = split(lt[...])

    each(YK, lambda j: v_copy(j).wait_recv())
    cross = dot3(lt_split, split(vall[...].reshape(512, NE)), NT)
    folded = jnp.zeros((OWN, 512), F32)
    lane_row = lane((OWN, 512)) % BLOCK
    for i in range(BLOCK):
        folded = folded + jnp.where(lane_row == i, cross[i * OWN : (i + 1) * OWN], 0.0)
    brs[r] = exact(jnp.concatenate([folded[0:8], folded[8:16]], axis=1), collect, NN)

    def b_copy(j):
        return send(brs.at[r], brs.at[r], s_b.at[j], r_b.at[j], row_peer(j))

    each(ROWS, lambda j: b_copy(j).start())
    each(ROWS, lambda j: b_copy(j).wait_recv())
    bias8 = 0.1 * jnp.sum(brs[...], axis=0)

    bias_wide = jnp.zeros((128, 128), F32)
    for s in range(2):
        pick = (full_lane == full_sub // 8 + W * s).astype(F32)
        place = (lane((8, 128)) % OWN == sub((8, 128)) + 8 * s).astype(F32)
        bias_wide = bias_wide + exact(exact(pick, bias8, NT), place, NN)
    field_wide = jnp.where(full_sub % 8 == full_lane // OWN, 0.1 * (noise_wide - bias_wide), 0.0)
    field_split = split(field_wide)
    for b in range(4):
        rows = slice(b * 128, (b + 1) * 128)
        part = dot3(field_split, (slab_top[rows, :], slab_low[rows, :]), NN)
        pot[:, b * 8 : (b + 1) * 8, :] = part.reshape(W, 8, M)

    def number(half, at_y, core):
        return half * YK + at_y * NK + core

    def k_copy(half, j):
        at_y = (y + j) % NY
        return send(
            pot.at[number(half, at_y, 1 - k)], rc.at[half, j], s_k.at[half, j], r_k.at[half, j], core_peer
        )

    def y_copy(half, j):
        return send(
            pot.at[number(half, (y + j) % NY, k)], ry.at[half, j], s_y.at[half, j], r_y.at[half, j], y_peer(j)
        )

    for half in (1 - h, h):
        each(NY, lambda j, half=half: k_copy(half, j).start())
        k_copy(half, 0).start()

    field8 = noise8 - bias8
    share = jnp.sum(field8 * bias8 - 0.5 * bias8 * bias8, axis=0, keepdims=True)
    lws[yk] = jnp.broadcast_to(share, (8, 128))

    def l_copy(j):
        return send(lws.at[yk], lws.at[yk], s_l.at[j], r_l.at[j], yk_peer(j))

    each(YK, lambda j: l_copy(j).start())

    def add_core(half, j):
        k_copy(half, j).wait_recv()
        mine = number(half, (y + j) % NY, k)
        pot[mine] = pot[mine] + rc[half, j]

    for half in (1 - h, h):

        def pass_on(j, half=half):
            add_core(half, j)
            y_copy(half, j).start()

        each(NY, pass_on)
        add_core(half, 0)

    def add_y(half):
        each(NY, lambda j: y_copy(half, j).wait_recv())
        mine = number(half, y, k)
        pot[mine] = (pot[mine] + ry[half, 1]) + (ry[half, 2] + ry[half, 3])

    add_y(1 - h)
    z_copy = send(pot.at[number(1 - h, y, k)], rz, s_z.at[0], r_z.at[0], h_peer)
    z_copy.start()
    add_y(h)

    each(YK, lambda j: l_copy(j).wait_recv())
    lwz[h] = jnp.sum(lws[...], axis=0)
    m_copy = send(lwz.at[h], lwz.at[h], s_m.at[0], r_m.at[0], h_peer)
    m_copy.start()

    z_copy.wait_recv()
    px[x] = pot[number(h, y, k)] + rz[...]

    def p_copy(j):
        return send(px.at[x], px.at[x], s_p.at[j], r_p.at[j], x_peer(j))

    each(NX, lambda j: p_copy(j).start())
    m_copy.wait_recv()
    total = lwz[0] + lwz[1]
    fold = (lane((W, 128)) % W == sub((W, 128))) & (lane((W, 128)) < 2 * W)
    weight[...] = exact(total, fold.astype(F32), NT)
    each(NX, lambda j: p_copy(j).wait_recv())
    pot_split = split(px[...].reshape(NE, M))

    sum_t = first
    for n in range(1, TAYLOR + 1):
        each(NZ, lambda j, n=n: t_copy(n - 1, j).wait_recv())
        term = jnp.concatenate([tbuf[n - 1, q] for q in range(NZ)], axis=1)
        term = dot3(split(term), pot_split, NT) / float(n)
        sum_t = sum_t + term
        if n < TAYLOR:
            tbuf[n, z] = term
            each(NZ, lambda j, n=n: t_copy(n, j).start())

    fx[x] = sum_t

    def f_copy(j):
        return send(fx.at[x], fx.at[x], s_f.at[j], r_f.at[j], x_peer(j))

    each(NX, lambda j: f_copy(j).start())

    each(ROWS, lambda j: c_copy(j).wait_send())
    each(NX, lambda j: w_copy(j).wait_send())
    each(ROWS, lambda j: a_copy(j).wait_send())
    for n in range(TAYLOR):
        each(NZ, lambda j, n=n: t_copy(n, j).wait_send())
    each(YK, lambda j: v_copy(j).wait_send())
    each(ROWS, lambda j: b_copy(j).wait_send())
    for half in (1 - h, h):
        k_copy(half, 0).wait_send()
        each(NY, lambda j, half=half: k_copy(half, j).wait_send())
        each(NY, lambda j, half=half: y_copy(half, j).wait_send())
    each(YK, lambda j: l_copy(j).wait_send())
    z_copy.wait_send()
    m_copy.wait_send()
    each(NX, lambda j: p_copy(j).wait_send())

    each(NX, lambda j: f_copy(j).wait_recv())
    turn[...] = jnp.transpose(fx[...].reshape(NE, NE))
    out[0] = turn[pl.ds(pl.multiple_of(x * BLOCK, BLOCK), BLOCK), :]
    each(NX, lambda j: f_copy(j).wait_send())


def body(walkers, trial, cholesky, noise):
    vmem = pl.BlockSpec(memory_space=pltpu.VMEM)
    dma = pltpu.SemaphoreType.DMA

    def pair(*shape):
        return [dma(shape), dma(shape)]

    propagated, weight = pl.pallas_call(
        kernel,
        name="step",
        out_shape=(jax.ShapeDtypeStruct((1, BLOCK, NE), F32), jax.ShapeDtypeStruct((8, W), F32)),
        in_specs=[vmem, vmem, pl.BlockSpec(memory_space=pl.ANY), vmem],
        out_specs=(vmem, vmem),
        scratch_shapes=[
            pltpu.VMEM((512, M), F32),
            pltpu.VMEM((512, M), BF16),
            pltpu.VMEM((512, M), BF16),
            pltpu.VMEM((512, NE), F32),
            pltpu.VMEM((NH * NE, NE), F32),
            pltpu.VMEM((ROWS, 8, NE), F32),
            pltpu.VMEM((ROWS, 8, NE), F32),
            pltpu.VMEM((NX, BLOCK, NE), F32),
            pltpu.VMEM((TAYLOR, NZ, BLOCK, NE), F32),
            pltpu.VMEM((YK, NH, BLOCK, NE), F32),
            pltpu.VMEM((ROWS, 8, 128), F32),
            pltpu.VMEM((W, BLOCK, M), F32),
            pltpu.VMEM((NH, NY, BLOCK, M), F32),
            pltpu.VMEM((NH, NY, BLOCK, M), F32),
            pltpu.VMEM((BLOCK, M), F32),
            pltpu.VMEM((NX, BLOCK, M), F32),
            pltpu.VMEM((NX, BLOCK, NE), F32),
            pltpu.VMEM((NE, NE), F32),
            pltpu.VMEM((YK, 8, 128), F32),
            pltpu.VMEM((NH, 8, 128), F32),
            dma((BLOCK,)),
            *pair(ROWS),
            *pair(ROWS),
            *pair(NX),
            *pair(TAYLOR, NZ),
            *pair(YK),
            *pair(ROWS),
            *pair(NH, NY),
            *pair(NH, NY),
            *pair(1),
            *pair(NX),
            *pair(NX),
            *pair(YK),
            *pair(1),
        ],
        compiler_params=pltpu.CompilerParams(collective_id=0, has_side_effects=True, vmem_limit_bytes=40 * 2**20),
    )(walkers, trial, cholesky, noise)
    return propagated, weight[0]


def solution(mesh):
    return jax.shard_map(
        body,
        mesh=mesh,
        in_specs=(P(None, "rows", None), P(), P("chol", "rows"), P(None, "chol")),
        out_specs=(P("chol", "rows", None), P()),
        check_vma=False,
    )
```

```python
import jax
import jax.numpy as jnp
from jax import lax
from jax.experimental import pallas as pl
from jax.experimental.pallas import tpu as pltpu
from jax.sharding import PartitionSpec as P

M = 1024
NE = 128
TAYLOR = 6
NX, NZ, NH, NY, NK = 4, 8, 2, 4, 2
ROWS = NX * NZ
YK = NY * NK
BLOCK = M // ROWS
PARTS = BLOCK // 8
W = 16
OWN = 16
F32 = jnp.float32
BF16 = jnp.bfloat16
MESH_ID = pl.DeviceIdType.MESH
NT = (((1,), (1,)), ((), ()))
NN = (((1,), (0,)), ((), ()))
TN = (((0,), (0,)), ((), ()))
STOP = 99


def exact(a, b, dims):
    return lax.dot_general(a, b, dims, precision=lax.Precision.HIGHEST, preferred_element_type=F32)


def split(a):
    top = a.astype(BF16)
    return top, (a - top.astype(F32)).astype(BF16)


def dot3(a, b, dims):
    def one(p, q):
        return lax.dot_general(p, q, dims, preferred_element_type=F32)

    return one(a[0], b[0]) + (one(a[0], b[1]) + one(a[1], b[0]))


def sub(index):
    return lax.broadcasted_iota(jnp.int32, index, 0)


def lane(index):
    return lax.broadcasted_iota(jnp.int32, index, 1)


def eliminate(mats):
    row8 = sub((8, NE))
    out = []
    for mat in mats:
        spread = [jnp.broadcast_to(mat[:, u : u + 1], (NE, NE)) for u in range(8)]
        small = [s[0:8] for s in spread]
        top = jnp.where(lane((8, NE)) < 8, (lane((8, NE)) == row8).astype(F32), mat[0:8])
        for t in range(8):
            inverse = 1.0 / jnp.broadcast_to(small[t][t : t + 1], (8, NE))
            pivot = small[t]
            for u in range(t + 1, 8):
                scaled = jnp.broadcast_to(small[u][t : t + 1], (8, NE)) * inverse
                small[u] = jnp.where(row8 == t, scaled, small[u] - pivot * scaled)
            scaled = jnp.broadcast_to(top[t : t + 1], (8, NE)) * inverse
            top = jnp.where(row8 == t, scaled, top - pivot * scaled)
        rest = jnp.where(lane((NE - 8, NE)) < 8, 0.0, mat[8:])
        for u in range(8):
            rest = rest - spread[u][8:] * top[u : u + 1]
        out.append(pltpu.roll(jnp.concatenate([rest, top], axis=0), NE - 8, 1))
    return tuple(out)


def kernel(
    walkers, trial, cholesky, noise, out, weight,
    own_w, own_t, tri, noi, slab, slab_top, slab_low, lt, cpart, crs, cag, wx, tbuf, vall, brs, pot, rc, ry, rz, px, ptop, plow, fx, turn, lws, lwz,
    sem_l, sem_i, s_c, r_c, s_a, r_a, s_w, r_w, s_t, r_t, s_v, r_v, s_b, r_b, s_k, r_k, s_y, r_y, s_z, r_z, s_p, r_p, s_f, r_f, s_l, r_l, s_m, r_m,
):
    r = lax.axis_index("rows")
    c = lax.axis_index("chol")
    x, z = r // NZ, r % NZ
    h, yk = c // YK, c % YK
    y, k = yk // NK, yk % NK
    ring = h * NZ + z
    pending = []
    owed = {}

    def place(at_x, at_z, at_h, at_yk):
        return (at_x * NZ + at_z, at_h * YK + at_yk)

    def row_peer(j):
        return ((r + j) % ROWS, c)

    def near_z(j):
        return (ring + (j + 3) % NZ - 3 + 2 * NZ) % (2 * NZ)

    def near_peer(e):
        at = near_z(e % NZ)
        return place((x + e // NZ) % NX, at % NZ, at // NZ, yk)

    def x_peer(j):
        return place((x + j) % NX, z, h, yk)

    def other_z(j):
        low = (z % 2 + j % 2) % 2
        mid = (z // 2 % 2 + j // 2 % 2) % 2
        return low + 2 * mid + 4 * ((z // 4 + j // 4) % 2)

    def z_peer(j):
        return place(x, other_z(j), h, yk)

    def yk_peer(j):
        return place(x, z, h, (yk + j) % YK)

    def y_peer(j):
        return place(x, z, h, ((y + j) % NY) * NK + k)

    core_peer = place(x, z, h, y * NK + (1 - k))
    h_peer = place(x, z, 1 - h, yk)

    def send(src, dst, ss, rs, dev):
        return pltpu.make_async_remote_copy(
            src_ref=src, dst_ref=dst, send_sem=ss, recv_sem=rs, device_id=dev, device_id_type=MESH_ID
        )

    def each(n, step, first=1):
        def run(j, carry):
            step(j)
            return carry

        lax.fori_loop(first, n, run, 0)

    def launch(name, n, copy, first=1, waits=True):
        each(n, lambda j: copy(j).start(), first)
        pending.append(lambda: each(n, lambda j: copy(j).wait_send(), first))
        owed[name] = lambda: each(n, lambda j: copy(j).wait_recv(), first)

    def arrive(name):
        owed.pop(name)()

    def finish():
        for name in list(owed):
            arrive(name)
        for wait in pending:
            wait()

    def aligned(start, size):
        return pl.ds(pl.multiple_of(start, size), size)

    def load(i):
        return pltpu.make_async_copy(
            cholesky.at[:, aligned(i * M, M)], slab.at[aligned(i * OWN, OWN)], sem_l.at[i]
        )

    first_loads = [
        pltpu.make_async_copy(trial.at[aligned(r * BLOCK, BLOCK)], own_t, sem_i.at[0]),
        pltpu.make_async_copy(walkers.at[yk], own_w.at[0], sem_i.at[1]),
        pltpu.make_async_copy(walkers.at[YK + yk], own_w.at[1], sem_i.at[2]),
    ]
    later_loads = [
        pltpu.make_async_copy(trial, tri, sem_i.at[3]),
        pltpu.make_async_copy(noise, noi, sem_i.at[4]),
        pltpu.make_async_copy(walkers.at[c], wx.at[x], sem_i.at[5]),
    ]
    for copy in first_loads:
        copy.start()

    barrier = pltpu.get_barrier_semaphore()

    def greet(dev):
        pl.semaphore_signal(barrier, inc=1, device_id=dev, device_id_type=MESH_ID)

    around = NX * 9

    def greet_near(e):
        at = (ring + e % 9 - 4 + 2 * NZ) % (2 * NZ)
        greet(place((x + e // 9) % NX, at % NZ, at // NZ, yk))

    each(4, greet_near, 0)
    each(around, greet_near, 5)
    each(YK, lambda j: greet(yk_peer(j)))
    each(BLOCK, lambda i: load(i).start(), 0)
    for copy in later_loads:
        copy.start()

    for copy in first_loads:
        copy.wait()
    for s in range(NH):
        cpart[s * NE : (s + 1) * NE, :] = exact(own_t[...], own_w[s], TN)

    pl.semaphore_wait(barrier, around - 1 + YK - 1)

    def c_copy(e):
        at = near_z(e % NZ) % NZ + NZ * ((x + e // NZ) % NX)
        return send(cpart.at[aligned(8 * at, 8)], crs.at[e], s_c.at[e], r_c.at[e], near_peer(e))

    launch("c", ROWS, c_copy)

    each(BLOCK, lambda i: load(i).wait(), 0)
    for copy in later_loads:
        copy.wait()
    trial_split = split(tri[...])

    def prepare(b):
        rows = aligned(b * 128, 128)
        block = slab[rows, :]
        top, low = split(block)
        lt[rows, :] = dot3((top, low), trial_split, NN)
        for t in range(NZ):
            at_tile, at_lane = t // 4, (t % 4) * BLOCK
            pieces = [
                block[:, (2 * q + at_tile) * 128 + at_lane : (2 * q + at_tile) * 128 + at_lane + BLOCK] for q in range(NX)
            ]
            top, low = split(jnp.concatenate(pieces, axis=1))
            slab_top[rows, t * 128 : (t + 1) * 128] = top
            slab_low[rows, t * 128 : (t + 1) * 128] = low

    each(4, prepare, 0)

    crs[0] = cpart[aligned(8 * r, 8), :]
    arrive("c")
    if STOP == 1:
        return finish()
    cag[r] = jnp.sum(crs[...], axis=0)
    launch("a", ROWS, lambda e: send(cag.at[r], cag.at[r], s_a.at[e], r_a.at[e], near_peer(e)))
    launch("w", NX, lambda j: send(wx.at[x], wx.at[x], s_w.at[j], r_w.at[j], x_peer(j)))

    full_sub, full_lane = sub((128, 128)), lane((128, 128))
    pick_w = (sub((128, W)) // 8 == lane((128, W))).astype(F32)
    pick_g = (lane((OWN, 128)) % OWN == sub((OWN, 128))).astype(F32)
    noise_wide = exact(exact(pick_w, noi[...], NN), pick_g, NN)
    own_group = lane((OWN, 128)) // W == sub((OWN, 128)) % 8
    spread_w = (lane((W, 128)) % W == sub((W, 128))).astype(F32)
    noise_rows = jnp.where(own_group, exact(noi[...], spread_w, TN), 0.0)
    noise2 = jnp.concatenate([jnp.sum(noise_rows[8 * a : 8 * a + 8], axis=0, keepdims=True) for a in range(2)], axis=0)
    rows512, lanes512 = sub((512, 128)), lane((512, 128))
    walker_of = ((rows512 // BLOCK) % NH) * YK + rows512 // (BLOCK * NH)
    collect = (lanes512 % W == walker_of).astype(F32)
    spread_g = sub((256, 128)) // 128 * 8 + (sub((256, 128)) % 128) // W == lane((256, 128)) % OWN
    spread_g = spread_g.astype(F32)
    lt_split = split(lt[...])

    arrive("w")
    turn[...] = jnp.transpose(wx[...].reshape(NE, NE))
    first = turn[aligned(x * BLOCK, BLOCK), :]
    tbuf[0, z] = first
    arrive("a")
    if STOP == 2:
        return finish()

    def t_copy(n):
        return lambda j: send(tbuf.at[n, z], tbuf.at[n, z], s_t.at[n, j], r_t.at[n, j], z_peer(j))

    launch("t0", NZ, t_copy(0))
    both = cag[...].reshape(NH * NE, NE)
    corr = [both[s * NE : (s + 1) * NE] for s in range(NH)]
    grams = tuple(exact(m, m, TN) for m in corr)
    inverses = lax.fori_loop(0, NE // 8, lambda i, m: eliminate(m), grams)
    for s in range(NH):
        left = exact(own_w[s], inverses[s], NN)
        vall[yk, s] = exact(left, corr[s], NT)
    if STOP == 3:
        return finish()
    launch("v", YK, lambda j: send(vall.at[yk], vall.at[yk], s_v.at[j], r_v.at[j], yk_peer(j)))
    arrive("v")
    if STOP == 4:
        return finish()

    cross = dot3(lt_split, split(vall[...].reshape(512, NE)), NT)
    folded = jnp.zeros((OWN, 512), F32)
    lane_row = lane((OWN, 512)) % BLOCK
    for i in range(BLOCK):
        folded = folded + jnp.where(lane_row == i, cross[i * OWN : (i + 1) * OWN], 0.0)
    share = jnp.where(own_group, exact(folded, collect, NN), 0.0)
    brs[r] = jnp.concatenate([jnp.sum(share[8 * a : 8 * a + 8], axis=0, keepdims=True) for a in range(2)], axis=0)
    launch("b", ROWS, lambda j: send(brs.at[r], brs.at[r], s_b.at[j], r_b.at[j], row_peer(j)))
    arrive("b")
    if STOP == 5:
        return finish()
    bias2 = 0.1 * jnp.sum(brs[...], axis=0)

    kept = full_lane % W == full_sub // 8
    picked = [jnp.where(kept, jnp.broadcast_to(bias2[a : a + 1], (128, 128)), 0.0) for a in range(2)]
    bias_wide = exact(jnp.concatenate(picked, axis=1), spread_g, NN)
    field_wide = jnp.where(full_sub % 8 == full_lane // OWN, 0.1 * (noise_wide - bias_wide), 0.0)
    field_split = split(field_wide)

    def number(half, at_y, core):
        return half * YK + at_y * NK + core

    def piece(ref, lead, p):
        return ref.at[(*lead, pl.ds(8 * p, 8))]

    def k_copy(half, p):
        def copy(j):
            src = piece(pot, (number(half, (y + j) % NY, 1 - k),), p)
            return send(src, piece(rc, (half, j), p), s_k.at[half, j, p], r_k.at[half, j, p], core_peer)

        return copy

    def y_copy(half, p):
        def copy(j):
            src = piece(pot, (number(half, (y + j) % NY, k),), p)
            return send(src, piece(ry, (half, j), p), s_y.at[half, j, p], r_y.at[half, j, p], y_peer(j))

        return copy

    for p in range(PARTS):
        rows = slice(p * 128, (p + 1) * 128)
        part = dot3(field_split, (slab_top[rows, :], slab_low[rows, :]), NN)
        pot[:, p * 8 : (p + 1) * 8, :] = part.reshape(W, 8, M)
        for half in (1 - h, h):
            each(NY, lambda j, half=half, p=p: k_copy(half, p)(j).start(), 0)
    for half in (1 - h, h):
        for p in range(PARTS):
            pending.append(lambda half=half, p=p: each(NY, lambda j: k_copy(half, p)(j).wait_send(), 0))

    field2 = noise2 - bias2
    lws[yk] = jnp.sum(field2 * bias2 - 0.5 * bias2 * bias2, axis=0, keepdims=True)
    launch("l", YK, lambda j: send(lws.at[yk], lws.at[yk], s_l.at[j], r_l.at[j], yk_peer(j)))

    def add_core(half, p, j):
        k_copy(half, p)(j).wait_recv()
        mine = number(half, (y + j) % NY, k)
        at = pl.ds(8 * p, 8)
        pot[mine, at] = pot[mine, at] + rc[half, j, at]

    for half in (1 - h, h):
        for p in range(PARTS):

            def pass_on(j, half=half, p=p):
                add_core(half, p, j)
                y_copy(half, p)(j).start()

            each(NY, pass_on)
            pending.append(lambda half=half, p=p: each(NY, lambda j: y_copy(half, p)(j).wait_send()))

    def add_y(half, p):
        add_core(half, p, 0)
        each(NY, lambda j: y_copy(half, p)(j).wait_recv())
        mine = number(half, y, k)
        at = pl.ds(8 * p, 8)
        pot[mine, at] = (pot[mine, at] + ry[half, 1, at]) + (ry[half, 2, at] + ry[half, 3, at])

    if STOP == 6:
        for half in (1 - h, h):
            for p in range(PARTS):
                add_y(half, p)
        return finish()

    def z_copy(p):
        src = piece(pot, (number(1 - h, y, k),), p)
        return send(src, piece(rz, (), p), s_z.at[p], r_z.at[p], h_peer)

    for p in range(PARTS):
        add_y(1 - h, p)
        z_copy(p).start()
        pending.append(lambda p=p: z_copy(p).wait_send())
    for p in range(PARTS):
        add_y(h, p)

    arrive("l")
    lwz[h] = jnp.sum(lws[...], axis=0)
    launch("m", 1, lambda j: send(lwz.at[h], lwz.at[h], s_m.at[0], r_m.at[0], h_peer), 0)

    def p_copy(p):
        def copy(j):
            ref = piece(px, (x,), p)
            return send(ref, ref, s_p.at[j, p], r_p.at[j, p], x_peer(j))

        return copy

    for p in range(PARTS):
        z_copy(p).wait_recv()
        at = slice(8 * p, 8 * p + 8)
        px[x, at] = pot[number(h, y, k), at] + rz[at]
        launch("p%d" % p, NX, p_copy(p))
    if STOP == 7:
        return finish()

    arrive("m")
    total = lwz[0] + lwz[1]
    fold = lane((W, 128)) % W == sub((W, 128))
    weight[...] = exact(jnp.broadcast_to(total, (8, 128)), fold.astype(F32), NT)[0:1]
    for p in range(PARTS):
        arrive("p%d" % p)
    if STOP == 8:
        return finish()
    pot_split = split(px[...].reshape(NE, M))
    for q in range(NZ):
        ptop[q] = pot_split[0][:, q * 128 : (q + 1) * 128]
        plow[q] = pot_split[1][:, q * 128 : (q + 1) * 128]

    sum_t = first
    for n in range(1, TAYLOR + 1):
        arrived = owed.pop("t%d" % (n - 1))
        del arrived
        term = jnp.zeros((BLOCK, NE), F32)
        for part in range(2):
            span = [other_z(4 * part + j) for j in range(4)]
            for j in range(4):
                if 4 * part + j:
                    t_copy(n - 1)(4 * part + j).wait_recv()
            held = split(jnp.concatenate([tbuf[n - 1, q] for q in span], axis=1))
            top = jnp.concatenate([ptop[q] for q in span], axis=1)
            low = jnp.concatenate([plow[q] for q in span], axis=1)
            term = term + dot3(held, (top, low), NT)
        term = term / float(n)
        sum_t = sum_t + term
        if n < TAYLOR:
            tbuf[n, z] = term
            launch("t%d" % n, NZ, lambda j, n=n: t_copy(n)((j + 2) % 7 + 1))
        if STOP == 8 + n:
            return finish()

    fx[x] = sum_t
    launch("f", NX, lambda j: send(fx.at[x], fx.at[x], s_f.at[j], r_f.at[j], x_peer(j)))
    arrive("f")
    turn[...] = jnp.transpose(fx[...].reshape(NE, NE))
    out[0] = turn[aligned(x * BLOCK, BLOCK), :]
    finish()


def call(walkers, trial, cholesky, noise, name="step", cid=0):
    vmem = pl.BlockSpec(memory_space=pltpu.VMEM)
    anywhere = pl.BlockSpec(memory_space=pl.ANY)
    dma = pltpu.SemaphoreType.DMA

    def pair(*shape):
        return [dma(shape), dma(shape)]

    propagated, weight = pl.pallas_call(
        kernel,
        name=name,
        out_shape=(jax.ShapeDtypeStruct((1, BLOCK, NE), F32), jax.ShapeDtypeStruct((1, W), F32)),
        in_specs=[anywhere] * 4,
        out_specs=(vmem, vmem),
        scratch_shapes=[
            pltpu.VMEM((NH, BLOCK, NE), F32),
            pltpu.VMEM((BLOCK, NE), F32),
            pltpu.VMEM((M, NE), F32),
            pltpu.VMEM((W, OWN), F32),
            pltpu.VMEM((512, M), F32),
            pltpu.VMEM((512, M), BF16),
            pltpu.VMEM((512, M), BF16),
            pltpu.VMEM((512, NE), F32),
            pltpu.VMEM((NH * NE, NE), F32),
            pltpu.VMEM((ROWS, 8, NE), F32),
            pltpu.VMEM((ROWS, 8, NE), F32),
            pltpu.VMEM((NX, BLOCK, NE), F32),
            pltpu.VMEM((TAYLOR, NZ, BLOCK, NE), F32),
            pltpu.VMEM((YK, NH, BLOCK, NE), F32),
            pltpu.VMEM((ROWS, 2, 128), F32),
            pltpu.VMEM((W, BLOCK, M), F32),
            pltpu.VMEM((NH, NY, BLOCK, M), F32),
            pltpu.VMEM((NH, NY, BLOCK, M), F32),
            pltpu.VMEM((BLOCK, M), F32),
            pltpu.VMEM((NX, BLOCK, M), F32),
            pltpu.VMEM((NZ, NE, 128), BF16),
            pltpu.VMEM((NZ, NE, 128), BF16),
            pltpu.VMEM((NX, BLOCK, NE), F32),
            pltpu.VMEM((NE, NE), F32),
            pltpu.VMEM((YK, 1, 128), F32),
            pltpu.VMEM((NH, 1, 128), F32),
            dma((BLOCK,)),
            dma((6,)),
            *pair(ROWS),
            *pair(ROWS),
            *pair(NX),
            *pair(TAYLOR, NZ),
            *pair(YK),
            *pair(ROWS),
            *pair(NH, NY, PARTS),
            *pair(NH, NY, PARTS),
            *pair(PARTS),
            *pair(NX, PARTS),
            *pair(NX),
            *pair(YK),
            *pair(1),
        ],
        compiler_params=pltpu.CompilerParams(collective_id=cid, has_side_effects=True, vmem_limit_bytes=60 * 2**20),
    )(walkers, trial, cholesky, noise)
    return propagated, weight.reshape(W)


def body(walkers, trial, cholesky, noise):
    return call(walkers, trial, cholesky, noise)


def solution(mesh):
    return jax.shard_map(
        body,
        mesh=mesh,
        in_specs=(P(None, "rows", None), P(), P("chol", "rows"), P(None, "chol")),
        out_specs=(P("chol", "rows", None), P()),
        check_vma=False,
    )
```

```python
import jax
import jax.numpy as jnp
from jax import lax
from jax.experimental import pallas as pl
from jax.experimental.pallas import tpu as pltpu
from jax.sharding import PartitionSpec as P

M = 1024
NE = 128
TAYLOR = 6
NX, NZ, NH, NY, NK = 4, 8, 2, 4, 2
ROWS = NX * NZ
YK = NY * NK
BLOCK = M // ROWS
PARTS = BLOCK // 8
W = 16
OWN = 16
F32 = jnp.float32
BF16 = jnp.bfloat16
MESH_ID = pl.DeviceIdType.MESH
NT = (((1,), (1,)), ((), ()))
NN = (((1,), (0,)), ((), ()))
TN = (((0,), (0,)), ((), ()))
AHEAD = 3
STOP = 99


def exact(a, b, dims):
    return lax.dot_general(a, b, dims, precision=lax.Precision.HIGHEST, preferred_element_type=F32)


def split(a):
    top = a.astype(BF16)
    return top, (a - top.astype(F32)).astype(BF16)


def dot3(a, b, dims):
    def one(p, q):
        return lax.dot_general(p, q, dims, preferred_element_type=F32)

    return one(a[0], b[0]) + (one(a[0], b[1]) + one(a[1], b[0]))


def sub(index):
    return lax.broadcasted_iota(jnp.int32, index, 0)


def lane(index):
    return lax.broadcasted_iota(jnp.int32, index, 1)


def pivot_block(mat, base):
    row8, lane8, lanes = sub((8, NE)), lane((8, NE)), lane((NE, NE))
    small = [jnp.broadcast_to(mat[base : base + 8, base + u : base + u + 1], (8, NE)) for u in range(8)]
    inside = (lane8 >= base) & (lane8 < base + 8)
    top = jnp.where(inside, (lane8 - base == row8).astype(F32), mat[base : base + 8])
    for t in range(8):
        inverse = 1.0 / jnp.broadcast_to(small[t][t : t + 1], (8, NE))
        pivot = small[t]
        for u in range(t + 1, 8):
            scaled = jnp.broadcast_to(small[u][t : t + 1], (8, NE)) * inverse
            small[u] = jnp.where(row8 == t, scaled, small[u] - pivot * scaled)
        scaled = jnp.broadcast_to(top[t : t + 1], (8, NE)) * inverse
        top = jnp.where(row8 == t, scaled, top - pivot * scaled)
    rest = jnp.where((lanes >= base) & (lanes < base + 8), 0.0, mat)
    rest = rest - exact(mat[:, base : base + 8], top, NN)
    above = [rest[:base]] if base else []
    return jnp.concatenate([*above, top, rest[base + 8 :]], axis=0)


def eliminate(mats):
    for q in range(4):
        mats = [pivot_block(mat, 8 * q) for mat in mats]
    return tuple(pltpu.roll(jnp.concatenate([m[32:], m[:32]], axis=0), NE - 32, 1) for m in mats)


def kernel(
    walkers, trial, cholesky, noise, out, weight,
    own_w, own_t, tri, noi, slab, slab_top, slab_low, lt, cpart, crs, cag, wz, tbuf, own_v, ball, brs, pot, rc, ry, pz, ptop, plow, fin, got, lws, lwz,
    sem_l, sem_i, s_c, r_c, s_a, r_a, s_w, r_w, s_t, r_t, s_g, r_g, s_h, r_h, s_v, r_v, s_b, r_b, s_k, r_k, s_y, r_y, s_z, r_z, s_f, r_f, s_l, r_l, s_m, r_m,
):
    r = lax.axis_index("rows")
    c = lax.axis_index("chol")
    x, z = r // NZ, r % NZ
    h, yk = c // YK, c % YK
    y, k = yk // NK, yk % NK
    ring = h * NZ + z
    goal = 2 + 4 * k
    at_goal = z == goal
    pending = []
    owed = {}

    def place(at_x, at_z, at_h, at_yk):
        return (at_x * NZ + at_z, at_h * YK + at_yk)

    def row_peer(e):
        return place((x + (e + 1) % NX) % NX, other_z(NZ - 1 - e // NX), h, yk)

    def near_z(e):
        at = e // NX
        return (ring + (1 - at % 2) * (4 - at // 2) + (at % 2) * (at // 2 - 3) + 2 * NZ) % (2 * NZ)

    def near_x(e):
        return (x + (e + 1) % NX) % NX

    def near_peer(e):
        return place(near_x(e), near_z(e) % NZ, near_z(e) // NZ, yk)

    def x_peer(j):
        return place((x + j) % NX, z, h, yk)

    def other_z(j):
        low = (z % 2 + j % 2) % 2
        mid = (z // 2 % 2 + j // 2 % 2) % 2
        return low + 2 * mid + 4 * ((z // 4 + j // 4) % 2)

    def z_peer(j):
        return place(x, other_z(j), h, yk)

    def yk_peer(j):
        return place(x, z, h, (yk + j) % YK)

    def y_peer(j):
        return place(x, z, h, ((y + j) % NY) * NK + k)

    core_peer = place(x, z, h, y * NK + (1 - k))
    h_peer = place(x, z, 1 - h, yk)

    def send(src, dst, ss, rs, dev):
        return pltpu.make_async_remote_copy(
            src_ref=src, dst_ref=dst, send_sem=ss, recv_sem=rs, device_id=dev, device_id_type=MESH_ID
        )

    def each(n, step, first=1):
        def run(j, carry):
            step(j)
            return carry

        lax.fori_loop(first, n, run, 0)

    def launch(name, n, copy, first=1, waits=True):
        each(n, lambda j: copy(j).start(), first)
        pending.append(lambda: each(n, lambda j: copy(j).wait_send(), first))
        owed[name] = lambda: each(n, lambda j: copy(j).wait_recv(), first)

    def arrive(name):
        owed.pop(name)()

    def finish():
        for name in list(owed):
            arrive(name)
        for wait in pending:
            wait()

    def aligned(start, size):
        return pl.ds(pl.multiple_of(start, size), size)

    def load(i):
        return pltpu.make_async_copy(
            cholesky.at[:, aligned(i * M, M)], slab.at[aligned(i * OWN, OWN)], sem_l.at[i]
        )

    first_loads = [
        pltpu.make_async_copy(trial.at[aligned(r * BLOCK, BLOCK)], own_t, sem_i.at[0]),
        pltpu.make_async_copy(walkers.at[yk], own_w.at[0], sem_i.at[1]),
        pltpu.make_async_copy(walkers.at[YK + yk], own_w.at[1], sem_i.at[2]),
    ]
    later_loads = [
        pltpu.make_async_copy(trial, tri, sem_i.at[3]),
        pltpu.make_async_copy(noise, noi, sem_i.at[4]),
        pltpu.make_async_copy(walkers.at[c], wz.at[z], sem_i.at[5]),
    ]
    for copy in first_loads:
        copy.start()

    barrier = pltpu.get_barrier_semaphore()

    def greet(dev):
        pl.semaphore_signal(barrier, inc=1, device_id=dev, device_id_type=MESH_ID)

    around = NX * 9

    def greet_near(e):
        at = (ring + e % 9 - 4 + 2 * NZ) % (2 * NZ)
        greet(place((x + e // 9) % NX, at % NZ, at // NZ, yk))

    each(4, greet_near, 0)
    each(around, greet_near, 5)
    each(YK, lambda j: greet(yk_peer(j)))
    each(BLOCK, lambda i: load(i).start(), 0)
    for copy in later_loads:
        copy.start()

    for copy in first_loads:
        copy.wait()
    for s in range(NH):
        cpart[s * NE : (s + 1) * NE, :] = exact(own_t[...], own_w[s], TN)

    pl.semaphore_wait(barrier, around - 1 + YK - 1)

    def c_copy(e):
        at = near_z(e) % NZ + NZ * near_x(e)
        return send(cpart.at[aligned(8 * at, 8)], crs.at[e], s_c.at[e], r_c.at[e], near_peer(e))

    launch("c", ROWS - 1, c_copy, 0)

    each(BLOCK, lambda i: load(i).wait(), 0)
    for copy in later_loads:
        copy.wait()
    trial_split = split(tri[...])

    def prepare(b):
        rows = aligned(b * 128, 128)
        block = slab[rows, :]
        top, low = split(block)
        lt[yk, rows, :] = dot3((top, low), trial_split, NN)
        slab_top[rows, :] = top
        slab_low[rows, :] = low

    each(4, prepare, 0)
    launch("g", NY, lambda j: send(lt.at[yk], lt.at[yk], s_g.at[j], r_g.at[j], y_peer(j)))

    def g_copy(j):
        ref = lt.at[(y + j) % NY * NK + k]
        return send(ref, ref, s_h.at[j], r_h.at[j], core_peer)

    launch("h0", 1, g_copy, 0)

    crs[ROWS - 1] = cpart[aligned(8 * r, 8), :]
    arrive("c")
    if STOP == 1:
        return finish()
    cag[r] = jnp.sum(crs[...], axis=0)
    launch("a", ROWS - 1, lambda e: send(cag.at[r], cag.at[r], s_a.at[e], r_a.at[e], near_peer(e)), 0)

    def w_copy(at):
        return send(wz.at[at], wz.at[at], s_w.at[0], r_w.at[at], place(x, goal, h, yk))

    @pl.when(jnp.logical_not(at_goal))
    def _():
        w_copy(z).start()

    full_sub, full_lane = sub((128, 128)), lane((128, 128))
    pick_w = (sub((128, W)) // 8 == lane((128, W))).astype(F32)
    pick_g = (lane((OWN, 128)) % OWN == sub((OWN, 128))).astype(F32)
    noise_wide = exact(exact(pick_w, noi[...], NN), pick_g, NN)
    own_g = (sub((128, 128)) // OWN == yk) & (sub((128, 128)) % OWN == lane((128, 128)) % OWN)
    own_g = own_g.astype(F32)
    same_g = (sub((128, 128)) % OWN == lane((128, 128)) % OWN).astype(F32)
    one_lane = (lane((8, 128)) < OWN).astype(F32)

    arrive("a")
    if STOP == 2:
        return finish()

    def t_copy(n):
        return lambda j: send(tbuf.at[n, x], tbuf.at[n, x], s_t.at[n, j], r_t.at[n, j], x_peer(j))

    @pl.when(at_goal)
    def _():
        each(NZ, lambda j: w_copy((z + j) % NZ).wait_recv())
        tbuf[0, x] = jnp.transpose(wz[...].reshape(NZ * BLOCK, NE))
        each(NX, lambda j: t_copy(0)(j).start())

    arrive("g")
    launch("h", NY, g_copy)
    both = cag[...].reshape(NH * NE, NE)
    corr = [both[s * NE : (s + 1) * NE] for s in range(NH)]
    grams = tuple(exact(m, m, TN) for m in corr)
    inverses = lax.fori_loop(0, NE // 32, lambda i, m: eliminate(m), grams)
    for s in range(NH):
        left = exact(own_w[s], inverses[s], NN)
        own_v[s * BLOCK : (s + 1) * BLOCK] = exact(left, corr[s], NT)
    arrive("h0")
    arrive("h")
    if STOP == 3:
        return finish()
    held_v = split(own_v[...])
    shares = []
    row_lane = lane((NH * BLOCK, 512)) // OWN == sub((NH * BLOCK, 512)) % BLOCK
    for q in range(YK):
        cross = jnp.where(row_lane, dot3(held_v, split(lt[q]), NT), 0.0)
        cross = (cross[:, 0:128] + cross[:, 128:256]) + (cross[:, 256:384] + cross[:, 384:512])
        shares.append([jnp.sum(cross[s * BLOCK : (s + 1) * BLOCK], axis=0, keepdims=True) for s in range(NH)])
    shares = jnp.concatenate([shares[q][s] for s in range(NH) for q in range(YK)], axis=0)
    shares = exact(shares, same_g, NN)
    shares = jnp.where(lane((W, 128)) // OWN == sub((W, 128)) % YK, shares, 0.0)
    brs[r] = jnp.concatenate([jnp.sum(shares[8 * a : 8 * a + 8], axis=0, keepdims=True) for a in range(2)], axis=0)
    launch("b", ROWS - 1, lambda e: send(brs.at[r], brs.at[r], s_b.at[e], r_b.at[e], row_peer(e)), 0)
    if STOP == 4:
        return finish()
    arrive("b")
    ball[yk] = 0.1 * jnp.sum(brs[...], axis=0)
    launch("v", YK, lambda j: send(ball.at[yk], ball.at[yk], s_v.at[j], r_v.at[j], yk_peer(j)))
    arrive("v")
    if STOP == 5:
        return finish()

    bias_rows = [jnp.broadcast_to(ball[q, s : s + 1], (8, 128)) for s in range(NH) for q in range(YK)]
    bias_wide = exact(jnp.concatenate(bias_rows, axis=0), own_g, NN)
    field_full = noise_wide - bias_wide
    field_wide = jnp.where(full_sub % 8 == full_lane // OWN, 0.1 * field_full, 0.0)
    field_split = split(field_wide)

    def number(half, at_y, core):
        return half * YK + at_y * NK + core

    def piece(ref, lead, p):
        return ref.at[(*lead, pl.ds(8 * p, 8))]

    def k_copy(half, p):
        def copy(j):
            src = piece(pot, (number(half, (y + j) % NY, 1 - k),), p)
            return send(src, piece(rc, (half, j), p), s_k.at[half, j, p], r_k.at[half, j, p], core_peer)

        return copy

    def y_copy(half, p):
        def copy(j):
            src = piece(pot, (number(half, (y + j) % NY, k),), p)
            return send(src, piece(ry, (half, j), p), s_y.at[half, j, p], r_y.at[half, j, p], y_peer(j))

        return copy

    for p in range(PARTS):
        rows = slice(p * 128, (p + 1) * 128)
        part = dot3(field_split, (slab_top[rows, :], slab_low[rows, :]), NN)
        pot[:, p * 8 : (p + 1) * 8, :] = part.reshape(W, 8, M)
        for half in (1 - h, h):
            each(NY, lambda j, half=half, p=p: k_copy(half, p)(j).start(), 0)
    for half in (1 - h, h):
        for p in range(PARTS):
            pending.append(lambda half=half, p=p: each(NY, lambda j: k_copy(half, p)(j).wait_send(), 0))

    exponent = field_full * bias_wide - 0.5 * bias_wide * bias_wide
    lws[yk] = exact(one_lane, exponent, NT)[0:1]
    launch("l", YK, lambda j: send(lws.at[yk], lws.at[yk], s_l.at[j], r_l.at[j], yk_peer(j)))

    def add_core(half, p, j):
        k_copy(half, p)(j).wait_recv()
        mine = number(half, (y + j) % NY, k)
        at = pl.ds(8 * p, 8)
        pot[mine, at] = pot[mine, at] + rc[half, j, at]

    def start_y(half, p):
        def pass_on(j):
            add_core(half, p, j)
            y_copy(half, p)(j).start()

        each(NY, pass_on)
        pending.append(lambda: each(NY, lambda j: y_copy(half, p)(j).wait_send()))

    def end_y(half, p):
        add_core(half, p, 0)
        each(NY, lambda j: y_copy(half, p)(j).wait_recv())
        mine = number(half, y, k)
        at = pl.ds(8 * p, 8)
        pot[mine, at] = (pot[mine, at] + ry[half, 1, at]) + (ry[half, 2, at] + ry[half, 3, at])

    def z_copy(half, p):
        src = piece(pot, (number(half, y, k),), p)
        return send(src, piece(pz, (ring,), p), s_z.at[half, p], r_z.at[ring, p], place(x, goal, half, yk))

    units = [(half, p) for p in range(PARTS) for half in (1 - h, h)]
    for unit in units[:AHEAD]:
        start_y(*unit)
    for at_unit, (half, p) in enumerate(units):
        end_y(half, p)
        if at_unit % 2 == 0:
            z_copy(half, p).start()
        else:

            @pl.when(jnp.logical_not(at_goal))
            def _(half=half, p=p):
                z_copy(half, p).start()

        if at_unit + AHEAD < len(units):
            start_y(*units[at_unit + AHEAD])

    arrive("l")
    lwz[h] = jnp.sum(lws[...], axis=0)
    launch("m", 1, lambda j: send(lwz.at[h], lwz.at[h], s_m.at[0], r_m.at[0], h_peer), 0)

    arrive("m")
    total = lwz[0] + lwz[1]
    fold = lane((W, 128)) == 8 * sub((W, 128))
    weight[...] = exact(jnp.broadcast_to(total, (8, 128)), fold.astype(F32), NT)[0:1]

    for p in range(PARTS):
        z_copy(1 - h, p).wait_send()

    @pl.when(jnp.logical_not(at_goal))
    def _():
        w_copy(z).wait_send()
        for p in range(PARTS):
            z_copy(h, p).wait_send()

    @pl.when(at_goal)
    def _():
        pz[ring] = pot[number(h, y, k)]

        def came(source, p):
            ref = piece(pz, (source,), p)
            send(ref, ref, s_z.at[0, p], r_z.at[source, p], h_peer).wait_recv()

        def assemble(j):
            row = (z + j) % NZ

            @pl.when(j > 0)
            def _():
                each(PARTS, lambda p: came(h * NZ + row, p), 0)

            each(PARTS, lambda p: came((1 - h) * NZ + row, p), 0)
            top, low = split(pz[row] + pz[NZ + row])
            rows = aligned(row * BLOCK, BLOCK)
            for q in range(NX):
                ptop[q, rows] = top[:, q * NZ * BLOCK : (q + 1) * NZ * BLOCK]
                plow[q, rows] = low[:, q * NZ * BLOCK : (q + 1) * NZ * BLOCK]

        each(NZ, assemble, 0)
        sum_t = tbuf[0, x]
        for n in range(1, TAYLOR + 1):
            term = jnp.zeros((NE, NZ * BLOCK), F32)
            if STOP >= 7 + n:
                for j in (0, 1, 3, 2):
                    if j:
                        t_copy(n - 1)(j).wait_recv()
                    at = (x + NX - j) % NX
                    term = term + dot3(split(tbuf[n - 1, at]), (ptop[at], plow[at]), NT)
                term = term / float(n)
                sum_t = sum_t + term
                if n < TAYLOR:
                    tbuf[n, x] = term
                    each(NX, lambda j, n=n: t_copy(n)(j).start())
            elif STOP == 6 + n:
                each(NX, lambda j, n=n: t_copy(n - 1)(j).wait_recv())
        fin[...] = jnp.transpose(sum_t).reshape(NZ, BLOCK, NE)

        def f_copy(j):
            return send(fin.at[(z + j) % NZ], got, s_f.at[j], r_f.at[0], place(x, (z + j) % NZ, h, yk))

        each(NZ, lambda j: f_copy(j).start())
        out[0] = fin[z]
        for n in range(min(TAYLOR, STOP - 6)):
            each(NX, lambda j, n=n: t_copy(n)(j).wait_send())
        each(NZ, lambda j: f_copy(j).wait_send())

    @pl.when(jnp.logical_not(at_goal))
    def _():
        send(fin.at[0], got, s_f.at[0], r_f.at[0], h_peer).wait_recv()
        out[0] = got[...]

    finish()


def call(walkers, trial, cholesky, noise, name="step", cid=0):
    vmem = pl.BlockSpec(memory_space=pltpu.VMEM)
    anywhere = pl.BlockSpec(memory_space=pltpu.HBM)
    dma = pltpu.SemaphoreType.DMA

    def pair(*shape):
        return [dma(shape), dma(shape)]

    propagated, weight = pl.pallas_call(
        kernel,
        name=name,
        out_shape=(jax.ShapeDtypeStruct((1, BLOCK, NE), F32), jax.ShapeDtypeStruct((1, W), F32)),
        in_specs=[anywhere] * 4,
        out_specs=(vmem, vmem),
        scratch_shapes=[
            pltpu.VMEM((NH, BLOCK, NE), F32),
            pltpu.VMEM((BLOCK, NE), F32),
            pltpu.VMEM((M, NE), F32),
            pltpu.VMEM((W, OWN), F32),
            pltpu.VMEM((512, M), F32),
            pltpu.VMEM((512, M), BF16),
            pltpu.VMEM((512, M), BF16),
            pltpu.VMEM((YK, 512, NE), F32),
            pltpu.VMEM((NH * NE, NE), F32),
            pltpu.VMEM((ROWS, 8, NE), F32),
            pltpu.VMEM((ROWS, 8, NE), F32),
            pltpu.VMEM((NZ, BLOCK, NE), F32),
            pltpu.VMEM((TAYLOR, NX, NE, NZ * BLOCK), F32),
            pltpu.VMEM((NH * BLOCK, NE), F32),
            pltpu.VMEM((YK, NH, 128), F32),
            pltpu.VMEM((ROWS, 2, 128), F32),
            pltpu.VMEM((W, BLOCK, M), F32),
            pltpu.VMEM((NH, NY, BLOCK, M), F32),
            pltpu.VMEM((NH, NY, BLOCK, M), F32),
            pltpu.VMEM((NH * NZ, BLOCK, M), F32),
            pltpu.VMEM((NX, NZ * BLOCK, NZ * BLOCK), BF16),
            pltpu.VMEM((NX, NZ * BLOCK, NZ * BLOCK), BF16),
            pltpu.VMEM((NZ, BLOCK, NE), F32),
            pltpu.VMEM((BLOCK, NE), F32),
            pltpu.VMEM((YK, 1, 128), F32),
            pltpu.VMEM((NH, 1, 128), F32),
            dma((BLOCK,)),
            dma((6,)),
            *pair(ROWS),
            *pair(ROWS),
            dma((1,)),
            dma((NZ,)),
            *pair(TAYLOR, NX),
            *pair(NY),
            *pair(NY),
            *pair(YK),
            *pair(ROWS),
            *pair(NH, NY, PARTS),
            *pair(NH, NY, PARTS),
            dma((NH, PARTS)),
            dma((NH * NZ, PARTS)),
            dma((NZ,)),
            dma((1,)),
            *pair(YK),
            *pair(1),
        ],
        compiler_params=pltpu.CompilerParams(collective_id=cid, has_side_effects=True, vmem_limit_bytes=60 * 2**20),
    )(walkers, trial, cholesky, noise)
    return propagated, weight.reshape(W)


def body(walkers, trial, cholesky, noise):
    return call(walkers, trial, cholesky, noise)


def solution(mesh):
    return jax.shard_map(
        body,
        mesh=mesh,
        in_specs=(P(None, "rows", None), P(), P("chol", "rows"), P(None, "chol")),
        out_specs=(P("chol", "rows", None), P()),
        check_vma=False,
    )
```

```python
import jax
import jax.numpy as jnp
from jax import lax
from jax.experimental import pallas as pl
from jax.experimental.pallas import tpu as pltpu
from jax.sharding import PartitionSpec as P

M = 1024
NE = 128
TAYLOR = 6
NX, NZ, NH, NY, NK = 4, 8, 2, 4, 2
ROWS = NX * NZ
YK = NY * NK
BLOCK = M // ROWS
PARTS = BLOCK // 8
W = 16
OWN = 16
F32 = jnp.float32
BF16 = jnp.bfloat16
MESH_ID = pl.DeviceIdType.MESH
NT = (((1,), (1,)), ((), ()))
NN = (((1,), (0,)), ((), ()))
TN = (((0,), (0,)), ((), ()))
AHEAD = 3
CHAINS = 2
STOP = 99


def exact(a, b, dims):
    return lax.dot_general(a, b, dims, precision=lax.Precision.HIGHEST, preferred_element_type=F32)


def split(a):
    top = a.astype(BF16)
    return top, (a - top.astype(F32)).astype(BF16)


def dot3(a, b, dims):
    def one(p, q):
        return lax.dot_general(p, q, dims, preferred_element_type=F32)

    return one(a[0], b[0]) + (one(a[0], b[1]) + one(a[1], b[0]))


def sub(index):
    return lax.broadcasted_iota(jnp.int32, index, 0)


def lane(index):
    return lax.broadcasted_iota(jnp.int32, index, 1)


def pivot_block(mat, base):
    row8, lane8, lanes = sub((8, NE)), lane((8, NE)), lane((NE, NE))
    small = [jnp.broadcast_to(mat[base : base + 8, base + u : base + u + 1], (8, NE)) for u in range(8)]
    inside = (lane8 >= base) & (lane8 < base + 8)
    top = jnp.where(inside, (lane8 - base == row8).astype(F32), mat[base : base + 8])
    for t in range(8):
        inverse = 1.0 / jnp.broadcast_to(small[t][t : t + 1], (8, NE))
        pivot = small[t]
        for u in range(t + 1, 8):
            scaled = jnp.broadcast_to(small[u][t : t + 1], (8, NE)) * inverse
            small[u] = jnp.where(row8 == t, scaled, small[u] - pivot * scaled)
        scaled = jnp.broadcast_to(top[t : t + 1], (8, NE)) * inverse
        top = jnp.where(row8 == t, scaled, top - pivot * scaled)
    rest = jnp.where((lanes >= base) & (lanes < base + 8), 0.0, mat)
    rest = rest - exact(mat[:, base : base + 8], top, NN)
    above = [rest[:base]] if base else []
    return jnp.concatenate([*above, top, rest[base + 8 :]], axis=0)


def eliminate(mats):
    for q in range(4):
        mats = [pivot_block(mat, 8 * q) for mat in mats]
    return tuple(pltpu.roll(jnp.concatenate([m[32:], m[:32]], axis=0), NE - 32, 1) for m in mats)


def kernel(
    walkers, trial, cholesky, noise, out, weight,
    own_w, own_t, tri, noi, slab, slab_top, slab_low, lt, cpart, crs, cag, wz, tbuf, own_v, ball, brs, pot, rc, ry, pz, ptop, plow, fin, got, lws, lwz,
    sem_l, sem_i, s_c, r_c, s_a, r_a, s_w, r_w, s_t, r_t, s_g, r_g, s_h, r_h, s_v, r_v, s_b, r_b, s_k, r_k, s_y, r_y, s_z, r_z, s_f, r_f, s_l, r_l, s_m, r_m,
):
    r = lax.axis_index("rows")
    c = lax.axis_index("chol")
    x, z = r // NZ, r % NZ
    h, yk = c // YK, c % YK
    y, k = yk // NK, yk % NK
    ring = h * NZ + z
    goal = 2 + 4 * k
    at_goal = z == goal
    pending = []
    owed = {}

    def place(at_x, at_z, at_h, at_yk):
        return (at_x * NZ + at_z, at_h * YK + at_yk)

    def row_peer(e):
        return place((x + (e + 1) % NX) % NX, other_z(NZ - 1 - e // NX), h, yk)

    def near_z(e):
        at = e // NX
        return (ring + (1 - at % 2) * (4 - at // 2) + (at % 2) * (at // 2 - 3) + 2 * NZ) % (2 * NZ)

    def near_x(e):
        return (x + (e + 1) % NX) % NX

    def near_peer(e):
        return place(near_x(e), near_z(e) % NZ, near_z(e) // NZ, yk)

    def x_peer(j):
        return place((x + j) % NX, z, h, yk)

    def other_z(j):
        low = (z % 2 + j % 2) % 2
        mid = (z // 2 % 2 + j // 2 % 2) % 2
        return low + 2 * mid + 4 * ((z // 4 + j // 4) % 2)

    def z_peer(j):
        return place(x, other_z(j), h, yk)

    def yk_peer(j):
        return place(x, z, h, (yk + j) % YK)

    def y_peer(j):
        return place(x, z, h, ((y + j) % NY) * NK + k)

    core_peer = place(x, z, h, y * NK + (1 - k))
    h_peer = place(x, z, 1 - h, yk)

    def send(src, dst, ss, rs, dev):
        return pltpu.make_async_remote_copy(
            src_ref=src, dst_ref=dst, send_sem=ss, recv_sem=rs, device_id=dev, device_id_type=MESH_ID
        )

    def each(n, step, first=1):
        def run(j, carry):
            step(j)
            return carry

        lax.fori_loop(first, n, run, 0)

    def launch(name, n, copy, first=1, waits=True):
        each(n, lambda j: copy(j).start(), first)
        pending.append(lambda: each(n, lambda j: copy(j).wait_send(), first))
        owed[name] = lambda: each(n, lambda j: copy(j).wait_recv(), first)

    def arrive(name):
        owed.pop(name)()

    def finish():
        for name in list(owed):
            arrive(name)
        for wait in pending:
            wait()

    def aligned(start, size):
        return pl.ds(pl.multiple_of(start, size), size)

    def load(i):
        return pltpu.make_async_copy(
            cholesky.at[:, aligned(i * M, M)], slab.at[aligned(i * OWN, OWN)], sem_l.at[i]
        )

    first_loads = [
        pltpu.make_async_copy(trial.at[aligned(r * BLOCK, BLOCK)], own_t, sem_i.at[0]),
        pltpu.make_async_copy(walkers.at[yk], own_w.at[0], sem_i.at[1]),
        pltpu.make_async_copy(walkers.at[YK + yk], own_w.at[1], sem_i.at[2]),
    ]
    later_loads = [
        pltpu.make_async_copy(trial, tri, sem_i.at[3]),
        pltpu.make_async_copy(noise, noi, sem_i.at[4]),
        pltpu.make_async_copy(walkers.at[c], wz.at[z], sem_i.at[5]),
    ]
    for copy in first_loads:
        copy.start()

    barrier = pltpu.get_barrier_semaphore()

    def greet(dev):
        pl.semaphore_signal(barrier, inc=1, device_id=dev, device_id_type=MESH_ID)

    around = NX * 9

    def greet_near(e):
        at = (ring + e % 9 - 4 + 2 * NZ) % (2 * NZ)
        greet(place((x + e // 9) % NX, at % NZ, at // NZ, yk))

    each(4, greet_near, 0)
    each(around, greet_near, 5)
    each(YK, lambda j: greet(yk_peer(j)))
    each(BLOCK, lambda i: load(i).start(), 0)
    for copy in later_loads:
        copy.start()

    for copy in first_loads:
        copy.wait()
    for s in range(NH):
        cpart[s * NE : (s + 1) * NE, :] = exact(own_t[...], own_w[s], TN)

    pl.semaphore_wait(barrier, around - 1 + YK - 1)

    def c_copy(e):
        at = near_z(e) % NZ + NZ * near_x(e)
        return send(cpart.at[aligned(8 * at, 8)], crs.at[e], s_c.at[e], r_c.at[e], near_peer(e))

    launch("c", ROWS - 1, c_copy, 0)

    each(BLOCK, lambda i: load(i).wait(), 0)
    for copy in later_loads:
        copy.wait()
    trial_split = split(tri[...])

    def prepare(b):
        rows = aligned(b * 128, 128)
        block = slab[rows, :]
        top, low = split(block)
        lt[yk, rows, :] = dot3((top, low), trial_split, NN)
        slab_top[rows, :] = top
        slab_low[rows, :] = low

    each(4, prepare, 0)
    launch("g", NY, lambda j: send(lt.at[yk], lt.at[yk], s_g.at[j], r_g.at[j], y_peer(j)))

    def g_copy(j):
        ref = lt.at[(y + j) % NY * NK + k]
        return send(ref, ref, s_h.at[j], r_h.at[j], core_peer)

    launch("h0", 1, g_copy, 0)

    crs[ROWS - 1] = cpart[aligned(8 * r, 8), :]
    arrive("c")
    if STOP == 1:
        return finish()
    cag[r] = jnp.sum(crs[...], axis=0)
    launch("a", ROWS - 1, lambda e: send(cag.at[r], cag.at[r], s_a.at[e], r_a.at[e], near_peer(e)), 0)

    def w_copy(at):
        return send(wz.at[at], wz.at[at], s_w.at[0], r_w.at[at], place(x, goal, h, yk))

    @pl.when(jnp.logical_not(at_goal))
    def _():
        w_copy(z).start()

    full_sub, full_lane = sub((128, 128)), lane((128, 128))
    pick_w = (sub((128, W)) // 8 == lane((128, W))).astype(F32)
    pick_g = (lane((OWN, 128)) % OWN == sub((OWN, 128))).astype(F32)
    noise_wide = exact(exact(pick_w, noi[...], NN), pick_g, NN)
    own_g = (sub((128, 128)) // OWN == yk) & (sub((128, 128)) % OWN == lane((128, 128)) % OWN)
    own_g = own_g.astype(F32)
    same_g = (sub((128, 128)) % OWN == lane((128, 128)) % OWN).astype(F32)
    one_lane = (lane((8, 128)) < OWN).astype(F32)

    arrive("a")
    if STOP == 2:
        return finish()

    def t_copy(n, q):
        def copy(j):
            ref = tbuf.at[n, x, pl.ds(q * (NE // CHAINS), NE // CHAINS)]
            return send(ref, ref, s_t.at[n, j, q], r_t.at[n, j, q], x_peer(j))

        return copy

    @pl.when(at_goal)
    def _():
        each(NZ, lambda j: w_copy((z + j) % NZ).wait_recv())
        tbuf[0, x] = jnp.transpose(wz[...].reshape(NZ * BLOCK, NE))
        for q in range(CHAINS):
            each(NX, lambda j, q=q: t_copy(0, q)(j).start())

    both = cag[...].reshape(NH * NE, NE)
    corr = [both[s * NE : (s + 1) * NE] for s in range(NH)]
    grams = tuple(exact(m, m, TN) for m in corr)
    inverses = lax.fori_loop(0, 2, lambda i, m: eliminate(m), grams)
    arrive("g")
    launch("h", NY, g_copy)
    inverses = lax.fori_loop(2, NE // 32, lambda i, m: eliminate(m), inverses)
    for s in range(NH):
        left = exact(own_w[s], inverses[s], NN)
        own_v[s * BLOCK : (s + 1) * BLOCK] = exact(left, corr[s], NT)
    arrive("h0")
    arrive("h")
    if STOP == 3:
        return finish()
    held_v = split(own_v[...])
    shares = []
    row_lane = lane((NH * BLOCK, 512)) // OWN == sub((NH * BLOCK, 512)) % BLOCK
    for q in range(YK):
        cross = jnp.where(row_lane, dot3(held_v, split(lt[q]), NT), 0.0)
        cross = (cross[:, 0:128] + cross[:, 128:256]) + (cross[:, 256:384] + cross[:, 384:512])
        shares.append([jnp.sum(cross[s * BLOCK : (s + 1) * BLOCK], axis=0, keepdims=True) for s in range(NH)])
    shares = jnp.concatenate([shares[q][s] for s in range(NH) for q in range(YK)], axis=0)
    shares = exact(shares, same_g, NN)
    shares = jnp.where(lane((W, 128)) // OWN == sub((W, 128)) % YK, shares, 0.0)
    brs[r] = jnp.concatenate([jnp.sum(shares[8 * a : 8 * a + 8], axis=0, keepdims=True) for a in range(2)], axis=0)
    launch("b", ROWS - 1, lambda e: send(brs.at[r], brs.at[r], s_b.at[e], r_b.at[e], row_peer(e)), 0)
    if STOP == 4:
        return finish()
    arrive("b")
    ball[yk] = 0.1 * jnp.sum(brs[...], axis=0)
    launch("v", YK, lambda j: send(ball.at[yk], ball.at[yk], s_v.at[j], r_v.at[j], yk_peer(j)))
    arrive("v")
    if STOP == 5:
        return finish()

    bias_rows = [jnp.broadcast_to(ball[q, s : s + 1], (8, 128)) for s in range(NH) for q in range(YK)]
    bias_wide = exact(jnp.concatenate(bias_rows, axis=0), own_g, NN)
    field_full = noise_wide - bias_wide
    field_wide = jnp.where(full_sub % 8 == full_lane // OWN, 0.1 * field_full, 0.0)
    field_split = split(field_wide)

    def number(half, at_y, core):
        return half * YK + at_y * NK + core

    def piece(ref, lead, p):
        return ref.at[(*lead, pl.ds(8 * p, 8))]

    def k_copy(half, p):
        def copy(j):
            src = piece(pot, (number(half, (y + j) % NY, 1 - k),), p)
            return send(src, piece(rc, (half, j), p), s_k.at[half, j, p], r_k.at[half, j, p], core_peer)

        return copy

    def y_copy(half, p):
        def copy(j):
            src = piece(pot, (number(half, (y + j) % NY, k),), p)
            return send(src, piece(ry, (half, j), p), s_y.at[half, j, p], r_y.at[half, j, p], y_peer(j))

        return copy

    for p in range(PARTS):
        rows = slice(p * 128, (p + 1) * 128)
        part = dot3(field_split, (slab_top[rows, :], slab_low[rows, :]), NN)
        pot[:, p * 8 : (p + 1) * 8, :] = part.reshape(W, 8, M)
        for half in (1 - h, h):
            each(NY, lambda j, half=half, p=p: k_copy(half, p)(j).start(), 0)
    for half in (1 - h, h):
        for p in range(PARTS):
            pending.append(lambda half=half, p=p: each(NY, lambda j: k_copy(half, p)(j).wait_send(), 0))

    exponent = field_full * bias_wide - 0.5 * bias_wide * bias_wide
    lws[yk] = exact(one_lane, exponent, NT)[0:1]
    launch("l", YK, lambda j: send(lws.at[yk], lws.at[yk], s_l.at[j], r_l.at[j], yk_peer(j)))

    def add_core(half, p, j):
        k_copy(half, p)(j).wait_recv()
        mine = number(half, (y + j) % NY, k)
        at = pl.ds(8 * p, 8)
        pot[mine, at] = pot[mine, at] + rc[half, j, at]

    def start_y(half, p):
        def pass_on(j):
            add_core(half, p, j)
            y_copy(half, p)(j).start()

        each(NY, pass_on)
        pending.append(lambda: each(NY, lambda j: y_copy(half, p)(j).wait_send()))

    def end_y(half, p):
        add_core(half, p, 0)
        each(NY, lambda j: y_copy(half, p)(j).wait_recv())
        mine = number(half, y, k)
        at = pl.ds(8 * p, 8)
        pot[mine, at] = (pot[mine, at] + ry[half, 1, at]) + (ry[half, 2, at] + ry[half, 3, at])

    def z_copy(half, p):
        src = piece(pot, (number(half, y, k),), p)
        return send(src, piece(pz, (ring,), p), s_z.at[half, p], r_z.at[ring, p], place(x, goal, half, yk))

    units = [(half, p) for p in range(PARTS) for half in (1 - h, h)]
    for unit in units[:AHEAD]:
        start_y(*unit)
    for at_unit, (half, p) in enumerate(units):
        end_y(half, p)
        if at_unit % 2 == 0:
            z_copy(half, p).start()
        else:

            @pl.when(jnp.logical_not(at_goal))
            def _(half=half, p=p):
                z_copy(half, p).start()

        if at_unit + AHEAD < len(units):
            start_y(*units[at_unit + AHEAD])

    arrive("l")
    lwz[h] = jnp.sum(lws[...], axis=0)
    launch("m", 1, lambda j: send(lwz.at[h], lwz.at[h], s_m.at[0], r_m.at[0], h_peer), 0)

    arrive("m")
    total = lwz[0] + lwz[1]
    fold = lane((W, 128)) == 8 * sub((W, 128))
    weight[...] = exact(jnp.broadcast_to(total, (8, 128)), fold.astype(F32), NT)[0:1]

    for p in range(PARTS):
        z_copy(1 - h, p).wait_send()

    @pl.when(jnp.logical_not(at_goal))
    def _():
        w_copy(z).wait_send()
        for p in range(PARTS):
            z_copy(h, p).wait_send()

    @pl.when(at_goal)
    def _():
        pz[ring] = pot[number(h, y, k)]

        def came(source, p):
            ref = piece(pz, (source,), p)
            send(ref, ref, s_z.at[0, p], r_z.at[source, p], h_peer).wait_recv()

        def assemble(j):
            row = (z + j) % NZ

            @pl.when(j > 0)
            def _():
                each(PARTS, lambda p: came(h * NZ + row, p), 0)

            each(PARTS, lambda p: came((1 - h) * NZ + row, p), 0)
            top, low = split(pz[row] + pz[NZ + row])
            rows = aligned(row * BLOCK, BLOCK)
            for q in range(NX):
                ptop[q, rows] = top[:, q * NZ * BLOCK : (q + 1) * NZ * BLOCK]
                plow[q, rows] = low[:, q * NZ * BLOCK : (q + 1) * NZ * BLOCK]

        each(NZ, assemble, 0)
        span = [slice(q * (NE // CHAINS), (q + 1) * (NE // CHAINS)) for q in range(CHAINS)]
        sums = [tbuf[0, x, span[q]] for q in range(CHAINS)]
        for n in range(1, min(TAYLOR, STOP - 7) + 1):
            for q in range(CHAINS):
                term = jnp.zeros((NE // CHAINS, NZ * BLOCK), F32)
                for j in (0, 1, 3, 2):
                    if j:
                        t_copy(n - 1, q)(j).wait_recv()
                    at = (x + NX - j) % NX
                    term = term + dot3(split(tbuf[n - 1, at, span[q]]), (ptop[at], plow[at]), NT)
                term = term / float(n)
                sums[q] = sums[q] + term
                if n < TAYLOR:
                    tbuf[n, x, span[q]] = term
                    for j in (2, 1, 3):
                        t_copy(n, q)(j).start()
        if STOP < 7 + TAYLOR:
            for q in range(CHAINS):
                each(NX, lambda j, q=q: t_copy(STOP - 7, q)(j).wait_recv())
        sum_t = jnp.concatenate(sums, axis=0)
        fin[...] = jnp.transpose(sum_t).reshape(NZ, BLOCK, NE)

        def f_copy(j):
            return send(fin.at[(z + j) % NZ], got, s_f.at[j], r_f.at[0], place(x, (z + j) % NZ, h, yk))

        each(NZ, lambda j: f_copy(j).start())
        out[0] = fin[z]
        for n in range(min(TAYLOR, STOP - 6)):
            for q in range(CHAINS):
                each(NX, lambda j, n=n, q=q: t_copy(n, q)(j).wait_send())
        each(NZ, lambda j: f_copy(j).wait_send())

    @pl.when(jnp.logical_not(at_goal))
    def _():
        send(fin.at[0], got, s_f.at[0], r_f.at[0], h_peer).wait_recv()
        out[0] = got[...]

    finish()


def call(walkers, trial, cholesky, noise, name="step", cid=0):
    vmem = pl.BlockSpec(memory_space=pltpu.VMEM)
    anywhere = pl.BlockSpec(memory_space=pltpu.HBM)
    dma = pltpu.SemaphoreType.DMA

    def pair(*shape):
        return [dma(shape), dma(shape)]

    propagated, weight = pl.pallas_call(
        kernel,
        name=name,
        out_shape=(jax.ShapeDtypeStruct((1, BLOCK, NE), F32), jax.ShapeDtypeStruct((1, W), F32)),
        in_specs=[anywhere] * 4,
        out_specs=(vmem, vmem),
        scratch_shapes=[
            pltpu.VMEM((NH, BLOCK, NE), F32),
            pltpu.VMEM((BLOCK, NE), F32),
            pltpu.VMEM((M, NE), F32),
            pltpu.VMEM((W, OWN), F32),
            pltpu.VMEM((512, M), F32),
            pltpu.VMEM((512, M), BF16),
            pltpu.VMEM((512, M), BF16),
            pltpu.VMEM((YK, 512, NE), F32),
            pltpu.VMEM((NH * NE, NE), F32),
            pltpu.VMEM((ROWS, 8, NE), F32),
            pltpu.VMEM((ROWS, 8, NE), F32),
            pltpu.VMEM((NZ, BLOCK, NE), F32),
            pltpu.VMEM((TAYLOR, NX, NE, NZ * BLOCK), F32),
            pltpu.VMEM((NH * BLOCK, NE), F32),
            pltpu.VMEM((YK, NH, 128), F32),
            pltpu.VMEM((ROWS, 2, 128), F32),
            pltpu.VMEM((W, BLOCK, M), F32),
            pltpu.VMEM((NH, NY, BLOCK, M), F32),
            pltpu.VMEM((NH, NY, BLOCK, M), F32),
            pltpu.VMEM((NH * NZ, BLOCK, M), F32),
            pltpu.VMEM((NX, NZ * BLOCK, NZ * BLOCK), BF16),
            pltpu.VMEM((NX, NZ * BLOCK, NZ * BLOCK), BF16),
            pltpu.VMEM((NZ, BLOCK, NE), F32),
            pltpu.VMEM((BLOCK, NE), F32),
            pltpu.VMEM((YK, 1, 128), F32),
            pltpu.VMEM((NH, 1, 128), F32),
            dma((BLOCK,)),
            dma((6,)),
            *pair(ROWS),
            *pair(ROWS),
            dma((1,)),
            dma((NZ,)),
            *pair(TAYLOR, NX, CHAINS),
            *pair(NY),
            *pair(NY),
            *pair(YK),
            *pair(ROWS),
            *pair(NH, NY, PARTS),
            *pair(NH, NY, PARTS),
            dma((NH, PARTS)),
            dma((NH * NZ, PARTS)),
            dma((NZ,)),
            dma((1,)),
            *pair(YK),
            *pair(1),
        ],
        compiler_params=pltpu.CompilerParams(collective_id=cid, has_side_effects=True, vmem_limit_bytes=60 * 2**20),
    )(walkers, trial, cholesky, noise)
    return propagated, weight.reshape(W)


def body(walkers, trial, cholesky, noise):
    return call(walkers, trial, cholesky, noise)


def solution(mesh):
    return jax.shard_map(
        body,
        mesh=mesh,
        in_specs=(P(None, "rows", None), P(), P("chol", "rows"), P(None, "chol")),
        out_specs=(P("chol", "rows", None), P()),
        check_vma=False,
    )
```

```python
import jax
import jax.numpy as jnp
from jax import lax
from jax.experimental import pallas as pl
from jax.experimental.pallas import tpu as pltpu
from jax.sharding import PartitionSpec as P

M = 1024
NE = 128
TAYLOR = 6
NX, NZ, NH, NY, NK = 4, 8, 2, 4, 2
ROWS = NX * NZ
YK = NY * NK
BLOCK = M // ROWS
PARTS = BLOCK // 8
W = 16
OWN = 16
F32 = jnp.float32
BF16 = jnp.bfloat16
MESH_ID = pl.DeviceIdType.MESH
NT = (((1,), (1,)), ((), ()))
NN = (((1,), (0,)), ((), ()))
TN = (((0,), (0,)), ((), ()))
AHEAD = 3
CHAINS = 2
STOP = 99


def exact(a, b, dims):
    return lax.dot_general(a, b, dims, precision=lax.Precision.HIGHEST, preferred_element_type=F32)


def split(a):
    top = a.astype(BF16)
    return top, (a - top.astype(F32)).astype(BF16)


def dot3(a, b, dims):
    def one(p, q):
        return lax.dot_general(p, q, dims, preferred_element_type=F32)

    return one(a[0], b[0]) + (one(a[0], b[1]) + one(a[1], b[0]))


def sub(index):
    return lax.broadcasted_iota(jnp.int32, index, 0)


def lane(index):
    return lax.broadcasted_iota(jnp.int32, index, 1)


def pivot_block(mat, base):
    row8, lane8, lanes = sub((8, NE)), lane((8, NE)), lane((NE, NE))

    def spread(rows):
        return [jnp.broadcast_to(rows[:, base + u : base + u + 1], (8, NE)) for u in range(8)]

    here, after = mat[base : base + 8], mat[base + 8 : base + 16]
    small, ahead = spread(here), spread(after)
    inside = (lane8 >= base) & (lane8 < base + 8)
    top = jnp.where(inside, (lane8 - base == row8).astype(F32), here)
    for t in range(8):
        inverse = 1.0 / jnp.broadcast_to(small[t][t : t + 1], (8, NE))
        pivot = small[t]
        for u in range(t + 1, 8):
            scaled = jnp.broadcast_to(small[u][t : t + 1], (8, NE)) * inverse
            small[u] = jnp.where(row8 == t, scaled, small[u] - pivot * scaled)
        scaled = jnp.broadcast_to(top[t : t + 1], (8, NE)) * inverse
        top = jnp.where(row8 == t, scaled, top - pivot * scaled)
    kept = jnp.where((lanes >= base) & (lanes < base + 8), 0.0, mat)
    rest = kept - exact(mat[:, base : base + 8], top, NN)
    part = [ahead[u] * top[u : u + 1] for u in range(8)]
    after = kept[base + 8 : base + 16] - (
        ((part[0] + part[1]) + (part[2] + part[3])) + ((part[4] + part[5]) + (part[6] + part[7]))
    )
    above = [rest[:base]] if base else []
    return jnp.concatenate([*above, top, after, rest[base + 16 :]], axis=0)


def eliminate(mats):
    for q in range(8):
        mats = [pivot_block(mat, 8 * q) for mat in mats]
    return tuple(pltpu.roll(jnp.concatenate([m[64:], m[:64]], axis=0), NE - 64, 1) for m in mats)


def kernel(
    walkers, trial, cholesky, noise, out, weight,
    own_w, own_t, tri, noi, slab, slab_top, slab_low, lt, cpart, crs, cag, wz, tbuf, own_v, ball, brs, pot, rc, ry, pz, ptop, plow, fin, got, lws, lwz,
    sem_l, sem_i, s_c, r_c, s_a, r_a, s_w, r_w, s_t, r_t, s_g, r_g, s_h, r_h, s_v, r_v, s_b, r_b, s_k, r_k, s_y, r_y, s_z, r_z, s_f, r_f, s_l, r_l, s_m, r_m,
):
    r = lax.axis_index("rows")
    c = lax.axis_index("chol")
    x, z = r // NZ, r % NZ
    h, yk = c // YK, c % YK
    y, k = yk // NK, yk % NK
    ring = h * NZ + z
    goal = 2 + 4 * k
    at_goal = z == goal
    pending = []
    owed = {}

    def place(at_x, at_z, at_h, at_yk):
        return (at_x * NZ + at_z, at_h * YK + at_yk)

    def row_peer(e):
        return place((x + (e + 1) % NX) % NX, other_z(NZ - 1 - e // NX), h, yk)

    def near_z(e):
        at = e // NX
        return (ring + (1 - at % 2) * (4 - at // 2) + (at % 2) * (at // 2 - 3) + 2 * NZ) % (2 * NZ)

    def near_x(e):
        return (x + (e + 1) % NX) % NX

    def near_peer(e):
        return place(near_x(e), near_z(e) % NZ, near_z(e) // NZ, yk)

    def x_peer(j):
        return place((x + j) % NX, z, h, yk)

    def other_z(j):
        low = (z % 2 + j % 2) % 2
        mid = (z // 2 % 2 + j // 2 % 2) % 2
        return low + 2 * mid + 4 * ((z // 4 + j // 4) % 2)

    def z_peer(j):
        return place(x, other_z(j), h, yk)

    def yk_peer(j):
        return place(x, z, h, (yk + j) % YK)

    def y_peer(j):
        return place(x, z, h, ((y + j) % NY) * NK + k)

    core_peer = place(x, z, h, y * NK + (1 - k))
    h_peer = place(x, z, 1 - h, yk)

    def send(src, dst, ss, rs, dev):
        return pltpu.make_async_remote_copy(
            src_ref=src, dst_ref=dst, send_sem=ss, recv_sem=rs, device_id=dev, device_id_type=MESH_ID
        )

    def each(n, step, first=1):
        def run(j, carry):
            step(j)
            return carry

        lax.fori_loop(first, n, run, 0)

    def launch(name, n, copy, first=1, waits=True):
        each(n, lambda j: copy(j).start(), first)
        pending.append(lambda: each(n, lambda j: copy(j).wait_send(), first))
        owed[name] = lambda: each(n, lambda j: copy(j).wait_recv(), first)

    def arrive(name):
        owed.pop(name)()

    def finish():
        for name in list(owed):
            arrive(name)
        for wait in pending:
            wait()

    def aligned(start, size):
        return pl.ds(pl.multiple_of(start, size), size)

    def load(i):
        return pltpu.make_async_copy(
            cholesky.at[:, aligned(i * M, M)], slab.at[aligned(i * OWN, OWN)], sem_l.at[i]
        )

    first_loads = [
        pltpu.make_async_copy(trial.at[aligned(r * BLOCK, BLOCK)], own_t, sem_i.at[0]),
        pltpu.make_async_copy(walkers.at[yk], own_w.at[0], sem_i.at[1]),
        pltpu.make_async_copy(walkers.at[YK + yk], own_w.at[1], sem_i.at[2]),
    ]
    later_loads = [
        pltpu.make_async_copy(trial, tri, sem_i.at[3]),
        pltpu.make_async_copy(noise, noi, sem_i.at[4]),
        pltpu.make_async_copy(walkers.at[c], wz.at[z], sem_i.at[5]),
    ]
    for copy in first_loads:
        copy.start()

    barrier = pltpu.get_barrier_semaphore()

    def greet(dev):
        pl.semaphore_signal(barrier, inc=1, device_id=dev, device_id_type=MESH_ID)

    around = NX * 9

    def greet_near(e):
        at = e // NX
        at = (ring + (1 - 2 * (at % 2)) * (4 - at // 2) + 2 * NZ) % (2 * NZ)
        greet(place((x + (e + 1) % NX) % NX, at % NZ, at // NZ, yk))

    each(around - 1, greet_near, 0)
    each(YK, lambda j: greet(yk_peer(j)))
    each(BLOCK, lambda i: load(i).start(), 0)
    for copy in later_loads:
        copy.start()

    for copy in first_loads:
        copy.wait()
    for s in range(NH):
        cpart[s * NE : (s + 1) * NE, :] = exact(own_t[...], own_w[s], TN)

    pl.semaphore_wait(barrier, around - 1 + YK - 1)

    def c_copy(e):
        at = near_z(e) % NZ + NZ * near_x(e)
        return send(cpart.at[aligned(8 * at, 8)], crs.at[e], s_c.at[e], r_c.at[e], near_peer(e))

    launch("c", ROWS - 1, c_copy, 0)

    each(BLOCK, lambda i: load(i).wait(), 0)
    for copy in later_loads:
        copy.wait()
    trial_split = split(tri[...])

    def prepare(b):
        rows = aligned(b * 128, 128)
        block = slab[rows, :]
        top, low = split(block)
        lt[yk, rows, :] = dot3((top, low), trial_split, NN)
        slab_top[rows, :] = top
        slab_low[rows, :] = low

    each(4, prepare, 0)
    launch("g", NY, lambda j: send(lt.at[yk], lt.at[yk], s_g.at[j], r_g.at[j], y_peer(j)))

    def g_copy(j):
        ref = lt.at[(y + j) % NY * NK + k]
        return send(ref, ref, s_h.at[j], r_h.at[j], core_peer)

    launch("h0", 1, g_copy, 0)

    crs[ROWS - 1] = cpart[aligned(8 * r, 8), :]
    arrive("c")
    if STOP == 1:
        return finish()
    cag[r] = jnp.sum(crs[...], axis=0)
    launch("a", ROWS - 1, lambda e: send(cag.at[r], cag.at[r], s_a.at[e], r_a.at[e], near_peer(e)), 0)

    def w_copy(at):
        return send(wz.at[at], wz.at[at], s_w.at[0], r_w.at[at], place(x, goal, h, yk))

    @pl.when(jnp.logical_not(at_goal))
    def _():
        w_copy(z).start()

    full_sub, full_lane = sub((128, 128)), lane((128, 128))
    pick_w = (sub((128, W)) // 8 == lane((128, W))).astype(F32)
    pick_g = (lane((OWN, 128)) % OWN == sub((OWN, 128))).astype(F32)
    noise_wide = exact(exact(pick_w, noi[...], NN), pick_g, NN)
    own_g = (sub((128, 128)) // OWN == yk) & (sub((128, 128)) % OWN == lane((128, 128)) % OWN)
    own_g = own_g.astype(F32)
    same_g = (sub((128, 128)) % OWN == lane((128, 128)) % OWN).astype(F32)
    one_lane = (lane((8, 128)) < OWN).astype(F32)

    arrive("a")
    if STOP == 2:
        return finish()

    def t_copy(n, q):
        def copy(j):
            ref = tbuf.at[n, x, pl.ds(q * (NE // CHAINS), NE // CHAINS)]
            return send(ref, ref, s_t.at[n, j, q], r_t.at[n, j, q], x_peer(j))

        return copy

    @pl.when(at_goal)
    def _():
        each(NZ, lambda j: w_copy((z + j) % NZ).wait_recv())
        tbuf[0, x] = jnp.transpose(wz[...].reshape(NZ * BLOCK, NE))
        for q in range(CHAINS):
            each(NX, lambda j, q=q: t_copy(0, q)(j).start())

    both = cag[...].reshape(NH * NE, NE)
    corr = [both[s * NE : (s + 1) * NE] for s in range(NH)]
    grams = tuple(exact(m, m, TN) for m in corr)

    def half_inverse(i, mats):
        @pl.when(i == 1)
        def _():
            arrive("g")
            launch("h", NY, g_copy)

        return eliminate(mats)

    inverses = lax.fori_loop(0, NE // 64, half_inverse, grams)
    for s in range(NH):
        left = exact(own_w[s], inverses[s], NN)
        own_v[s * BLOCK : (s + 1) * BLOCK] = exact(left, corr[s], NT)
    arrive("h0")
    arrive("h")
    if STOP == 3:
        return finish()
    held_v = split(own_v[...])
    shares = []
    row_lane = lane((NH * BLOCK, 512)) // OWN == sub((NH * BLOCK, 512)) % BLOCK
    for q in range(YK):
        cross = jnp.where(row_lane, dot3(held_v, split(lt[q]), NT), 0.0)
        cross = (cross[:, 0:128] + cross[:, 128:256]) + (cross[:, 256:384] + cross[:, 384:512])
        shares.append([jnp.sum(cross[s * BLOCK : (s + 1) * BLOCK], axis=0, keepdims=True) for s in range(NH)])
    shares = jnp.concatenate([shares[q][s] for s in range(NH) for q in range(YK)], axis=0)
    shares = exact(shares, same_g, NN)
    shares = jnp.where(lane((W, 128)) // OWN == sub((W, 128)) % YK, shares, 0.0)
    brs[r] = jnp.concatenate([jnp.sum(shares[8 * a : 8 * a + 8], axis=0, keepdims=True) for a in range(2)], axis=0)
    launch("b", ROWS - 1, lambda e: send(brs.at[r], brs.at[r], s_b.at[e], r_b.at[e], row_peer(e)), 0)
    if STOP == 4:
        return finish()
    arrive("b")
    ball[yk] = 0.1 * jnp.sum(brs[...], axis=0)
    launch("v", YK, lambda j: send(ball.at[yk], ball.at[yk], s_v.at[j], r_v.at[j], yk_peer(j)))
    arrive("v")
    if STOP == 5:
        return finish()

    bias_rows = [jnp.broadcast_to(ball[q, s : s + 1], (8, 128)) for s in range(NH) for q in range(YK)]
    bias_wide = exact(jnp.concatenate(bias_rows, axis=0), own_g, NN)
    field_full = noise_wide - bias_wide
    field_wide = jnp.where(full_sub % 8 == full_lane // OWN, 0.1 * field_full, 0.0)
    field_split = split(field_wide)

    def number(half, at_y, core):
        return half * YK + at_y * NK + core

    def piece(ref, lead, p):
        return ref.at[(*lead, pl.ds(8 * p, 8))]

    def k_copy(half, p):
        def copy(j):
            src = piece(pot, (number(half, (y + j) % NY, 1 - k),), p)
            return send(src, piece(rc, (half, j), p), s_k.at[half, j, p], r_k.at[half, j, p], core_peer)

        return copy

    def y_copy(half, p):
        def copy(j):
            src = piece(pot, (number(half, (y + j) % NY, k),), p)
            return send(src, piece(ry, (half, j), p), s_y.at[half, j, p], r_y.at[half, j, p], y_peer(j))

        return copy

    def add_core(half, p, j):
        k_copy(half, p)(j).wait_recv()
        mine = number(half, (y + j) % NY, k)
        at = pl.ds(8 * p, 8)
        pot[mine, at] = pot[mine, at] + rc[half, j, at]

    def start_y(half, p):
        def pass_on(j):
            add_core(half, p, j)
            y_copy(half, p)(j).start()

        each(NY, pass_on)
        pending.append(lambda: each(NY, lambda j: y_copy(half, p)(j).wait_send()))

    def end_y(half, p):
        add_core(half, p, 0)
        each(NY, lambda j: y_copy(half, p)(j).wait_recv())
        mine = number(half, y, k)
        at = pl.ds(8 * p, 8)
        pot[mine, at] = (pot[mine, at] + ry[half, 1, at]) + (ry[half, 2, at] + ry[half, 3, at])

    def z_copy(half, p):
        src = piece(pot, (number(half, y, k),), p)
        return send(src, piece(pz, (ring,), p), s_z.at[half, p], r_z.at[ring, p], place(x, goal, half, yk))

    units = [(half, p) for p in range(PARTS) for half in (1 - h, h)]
    for p in range(PARTS):
        rows = slice(p * 128, (p + 1) * 128)
        part = dot3(field_split, (slab_top[rows, :], slab_low[rows, :]), NN)
        pot[:, p * 8 : (p + 1) * 8, :] = part.reshape(W, 8, M)
        for half in (1 - h, h):
            each(NY, lambda j, half=half, p=p: k_copy(half, p)(j).start(), 0)
        if p:
            for unit in units[2 * p - 2 : min(2 * p, AHEAD)]:
                start_y(*unit)
    for half in (1 - h, h):
        for p in range(PARTS):
            pending.append(lambda half=half, p=p: each(NY, lambda j: k_copy(half, p)(j).wait_send(), 0))


    exponent = field_full * bias_wide - 0.5 * bias_wide * bias_wide
    lws[yk] = exact(one_lane, exponent, NT)[0:1]
    launch("l", YK, lambda j: send(lws.at[yk], lws.at[yk], s_l.at[j], r_l.at[j], yk_peer(j)))

    for at_unit, (half, p) in enumerate(units):
        end_y(half, p)
        if at_unit % 2 == 0:
            z_copy(half, p).start()
        else:

            @pl.when(jnp.logical_not(at_goal))
            def _(half=half, p=p):
                z_copy(half, p).start()

        if at_unit + AHEAD < len(units):
            start_y(*units[at_unit + AHEAD])

    arrive("l")
    lwz[h] = jnp.sum(lws[...], axis=0)
    launch("m", 1, lambda j: send(lwz.at[h], lwz.at[h], s_m.at[0], r_m.at[0], h_peer), 0)

    arrive("m")
    total = lwz[0] + lwz[1]
    fold = lane((W, 128)) == 8 * sub((W, 128))
    weight[...] = exact(jnp.broadcast_to(total, (8, 128)), fold.astype(F32), NT)[0:1]

    @pl.when(at_goal)
    def _():
        pz[ring] = pot[number(h, y, k)]

        def came(source, p):
            ref = piece(pz, (source,), p)
            send(ref, ref, s_z.at[0, p], r_z.at[source, p], h_peer).wait_recv()

        def assemble(j):
            row = (z + j) % NZ

            @pl.when(j > 0)
            def _():
                each(PARTS, lambda p: came(h * NZ + row, p), 0)

            each(PARTS, lambda p: came((1 - h) * NZ + row, p), 0)
            top, low = split(pz[row] + pz[NZ + row])
            rows = aligned(row * BLOCK, BLOCK)
            for q in range(NX):
                ptop[q, rows] = top[:, q * NZ * BLOCK : (q + 1) * NZ * BLOCK]
                plow[q, rows] = low[:, q * NZ * BLOCK : (q + 1) * NZ * BLOCK]

        each(NZ, assemble, 0)
        span = [slice(q * (NE // CHAINS), (q + 1) * (NE // CHAINS)) for q in range(CHAINS)]
        sums = [tbuf[0, x, span[q]] for q in range(CHAINS)]
        for n in range(1, min(TAYLOR, STOP - 7) + 1):
            for q in range(CHAINS):
                term = jnp.zeros((NE // CHAINS, NZ * BLOCK), F32)
                for j in (0, 1, 3, 2):
                    if j:
                        t_copy(n - 1, q)(j).wait_recv()
                    at = (x + NX - j) % NX
                    term = term + dot3(split(tbuf[n - 1, at, span[q]]), (ptop[at], plow[at]), NT)
                term = term / float(n)
                sums[q] = sums[q] + term
                if n < TAYLOR:
                    tbuf[n, x, span[q]] = term
                    for j in (2, 1, 3):
                        t_copy(n, q)(j).start()
        if STOP < 7 + TAYLOR:
            for q in range(CHAINS):
                each(NX, lambda j, q=q: t_copy(STOP - 7, q)(j).wait_recv())
        sum_t = jnp.concatenate(sums, axis=0)
        fin[...] = jnp.transpose(sum_t).reshape(NZ, BLOCK, NE)

        def f_copy(j):
            return send(fin.at[(z + j) % NZ], got, s_f.at[j], r_f.at[0], place(x, (z + j) % NZ, h, yk))

        each(NZ, lambda j: f_copy(j).start())
        out[0] = fin[z]
        for n in range(min(TAYLOR, STOP - 6)):
            for q in range(CHAINS):
                each(NX, lambda j, n=n, q=q: t_copy(n, q)(j).wait_send())
        each(NZ, lambda j: f_copy(j).wait_send())

    @pl.when(jnp.logical_not(at_goal))
    def _():
        send(fin.at[0], got, s_f.at[0], r_f.at[0], h_peer).wait_recv()
        out[0] = got[...]

    for p in range(PARTS):
        z_copy(1 - h, p).wait_send()

    @pl.when(jnp.logical_not(at_goal))
    def _():
        w_copy(z).wait_send()
        for p in range(PARTS):
            z_copy(h, p).wait_send()

    finish()


def hand_over(propagated, weight, propagated_out, weight_out, sems):
    copies = [
        pltpu.make_async_copy(propagated, propagated_out, sems.at[0]),
        pltpu.make_async_copy(weight.at[0], weight_out, sems.at[1]),
    ]
    for copy in copies:
        copy.start()
    for copy in copies:
        copy.wait()


def call(walkers, trial, cholesky, noise, name="step", cid=0):
    vmem = pl.BlockSpec(memory_space=pltpu.VMEM)
    anywhere = pl.BlockSpec(memory_space=pltpu.HBM)
    dma = pltpu.SemaphoreType.DMA

    def pair(*shape):
        return [dma(shape), dma(shape)]

    propagated, weight = pl.pallas_call(
        kernel,
        name=name,
        out_shape=(jax.ShapeDtypeStruct((1, BLOCK, NE), F32), jax.ShapeDtypeStruct((1, W), F32)),
        in_specs=[anywhere] * 4,
        out_specs=(vmem, vmem),
        scratch_shapes=[
            pltpu.VMEM((NH, BLOCK, NE), F32),
            pltpu.VMEM((BLOCK, NE), F32),
            pltpu.VMEM((M, NE), F32),
            pltpu.VMEM((W, OWN), F32),
            pltpu.VMEM((512, M), F32),
            pltpu.VMEM((512, M), BF16),
            pltpu.VMEM((512, M), BF16),
            pltpu.VMEM((YK, 512, NE), F32),
            pltpu.VMEM((NH * NE, NE), F32),
            pltpu.VMEM((ROWS, 8, NE), F32),
            pltpu.VMEM((ROWS, 8, NE), F32),
            pltpu.VMEM((NZ, BLOCK, NE), F32),
            pltpu.VMEM((TAYLOR, NX, NE, NZ * BLOCK), F32),
            pltpu.VMEM((NH * BLOCK, NE), F32),
            pltpu.VMEM((YK, NH, 128), F32),
            pltpu.VMEM((ROWS, 2, 128), F32),
            pltpu.VMEM((W, BLOCK, M), F32),
            pltpu.VMEM((NH, NY, BLOCK, M), F32),
            pltpu.VMEM((NH, NY, BLOCK, M), F32),
            pltpu.VMEM((NH * NZ, BLOCK, M), F32),
            pltpu.VMEM((NX, NZ * BLOCK, NZ * BLOCK), BF16),
            pltpu.VMEM((NX, NZ * BLOCK, NZ * BLOCK), BF16),
            pltpu.VMEM((NZ, BLOCK, NE), F32),
            pltpu.VMEM((BLOCK, NE), F32),
            pltpu.VMEM((YK, 1, 128), F32),
            pltpu.VMEM((NH, 1, 128), F32),
            dma((BLOCK,)),
            dma((6,)),
            *pair(ROWS),
            *pair(ROWS),
            dma((1,)),
            dma((NZ,)),
            *pair(TAYLOR, NX, CHAINS),
            *pair(NY),
            *pair(NY),
            *pair(YK),
            *pair(ROWS),
            *pair(NH, NY, PARTS),
            *pair(NH, NY, PARTS),
            dma((NH, PARTS)),
            dma((NH * NZ, PARTS)),
            dma((NZ,)),
            dma((1,)),
            *pair(YK),
            *pair(1),
        ],
        compiler_params=pltpu.CompilerParams(collective_id=cid, has_side_effects=True, vmem_limit_bytes=215 * 2**18),
    )(walkers, trial, cholesky, noise)
    return pl.pallas_call(
        hand_over,
        name="hand_over",
        out_shape=(jax.ShapeDtypeStruct((1, BLOCK, NE), F32), jax.ShapeDtypeStruct((W,), F32)),
        in_specs=[pl.BlockSpec(memory_space=pl.ANY)] * 2,
        out_specs=(pl.BlockSpec(memory_space=pl.ANY), pl.BlockSpec(memory_space=pl.ANY)),
        scratch_shapes=[dma((2,))],
        compiler_params=pltpu.CompilerParams(vmem_limit_bytes=2**20),
    )(propagated, weight)


def body(walkers, trial, cholesky, noise):
    return call(walkers, trial, cholesky, noise)


def solution(mesh):
    return jax.shard_map(
        body,
        mesh=mesh,
        in_specs=(P(None, "rows", None), P(), P("chol", "rows"), P(None, "chol")),
        out_specs=(P("chol", "rows", None), P()),
        check_vma=False,
    )
```

```python
import jax
import jax.numpy as jnp
from jax import lax
from jax.experimental import pallas as pl
from jax.experimental.pallas import tpu as pltpu
from jax.sharding import PartitionSpec as P

M = 1024
NE = 128
TAYLOR = 6
NX, NZ, NH, NY, NK = 4, 8, 2, 4, 2
ROWS = NX * NZ
YK = NY * NK
BLOCK = M // ROWS
PARTS = BLOCK // 8
W = 16
OWN = 16
F32 = jnp.float32
BF16 = jnp.bfloat16
MESH_ID = pl.DeviceIdType.MESH
NT = (((1,), (1,)), ((), ()))
NN = (((1,), (0,)), ((), ()))
TN = (((0,), (0,)), ((), ()))
AHEAD = 3
CHAINS = 4


def exact(a, b, dims):
    return lax.dot_general(a, b, dims, precision=lax.Precision.HIGHEST, preferred_element_type=F32)


def split(a):
    top = a.astype(BF16)
    return top, (a - top.astype(F32)).astype(BF16)


def dot3(a, b, dims):
    def one(p, q):
        return lax.dot_general(p, q, dims, preferred_element_type=F32)

    rows = a[0].shape[0]
    both = one(jnp.concatenate(a, axis=0), b[0])
    return both[:rows] + (one(a[0], b[1]) + both[rows:])


def sub(index):
    return lax.broadcasted_iota(jnp.int32, index, 0)


def lane(index):
    return lax.broadcasted_iota(jnp.int32, index, 1)


def pivot_block(mat, base):
    row8, lane8, lanes = sub((8, NE)), lane((8, NE)), lane((NE, NE))

    def spread(rows):
        return [jnp.broadcast_to(rows[:, base + u : base + u + 1], (8, NE)) for u in range(8)]

    here, after = mat[base : base + 8], mat[base + 8 : base + 16]
    small, ahead = spread(here), spread(after)
    inside = (lane8 >= base) & (lane8 < base + 8)
    top = jnp.where(inside, (lane8 - base == row8).astype(F32), here)
    for t in range(8):
        inverse = 1.0 / jnp.broadcast_to(small[t][t : t + 1], (8, NE))
        pivot = small[t]
        for u in range(t + 1, 8):
            scaled = jnp.broadcast_to(small[u][t : t + 1], (8, NE)) * inverse
            small[u] = jnp.where(row8 == t, scaled, small[u] - pivot * scaled)
        scaled = jnp.broadcast_to(top[t : t + 1], (8, NE)) * inverse
        top = jnp.where(row8 == t, scaled, top - pivot * scaled)
    kept = jnp.where((lanes >= base) & (lanes < base + 8), 0.0, mat)
    rest = kept - exact(mat[:, base : base + 8], top, NN)
    part = [ahead[u] * top[u : u + 1] for u in range(8)]
    after = kept[base + 8 : base + 16] - (
        ((part[0] + part[1]) + (part[2] + part[3])) + ((part[4] + part[5]) + (part[6] + part[7]))
    )
    above = [rest[:base]] if base else []
    return jnp.concatenate([*above, top, after, rest[base + 16 :]], axis=0)


def eliminate(mats):
    for q in range(8):
        mats = [pivot_block(mat, 8 * q) for mat in mats]
    return tuple(pltpu.roll(jnp.concatenate([m[64:], m[:64]], axis=0), NE - 64, 1) for m in mats)


def kernel(
    walkers, trial, cholesky, noise, out, weight,
    own_w, own_t, tri, noi, slab, slab_top, slab_low, lt, cpart, crs, cag, wz, tbuf, own_v, ball, brs, pot, rc, ry, pz, ptop, plow, fin, got, lws, lwz,
    sem_l, sem_i, s_c, r_c, s_a, r_a, s_w, r_w, s_t, r_t, s_g, r_g, s_h, r_h, s_v, r_v, s_b, r_b, s_k, r_k, s_y, r_y, s_z, r_z, s_f, r_f, s_l, r_l, s_m, r_m,
):
    r = lax.axis_index("rows")
    c = lax.axis_index("chol")
    x, z = r // NZ, r % NZ
    h, yk = c // YK, c % YK
    y, k = yk // NK, yk % NK
    ring = h * NZ + z
    goal = 2 + 4 * k
    at_goal = z == goal
    pending = []
    owed = {}

    def place(at_x, at_z, at_h, at_yk):
        return (at_x * NZ + at_z, at_h * YK + at_yk)

    def row_peer(e):
        return place((x + (e + 1) % NX) % NX, other_z(NZ - 1 - e // NX), h, yk)

    def near_z(e):
        at = e // NX
        return (ring + (1 - at % 2) * (4 - at // 2) + (at % 2) * (at // 2 - 3) + 2 * NZ) % (2 * NZ)

    def near_x(e):
        return (x + (e + 1) % NX) % NX

    def near_peer(e):
        return place(near_x(e), near_z(e) % NZ, near_z(e) // NZ, yk)

    def x_peer(j):
        return place((x + j) % NX, z, h, yk)

    def other_z(j):
        low = (z % 2 + j % 2) % 2
        mid = (z // 2 % 2 + j // 2 % 2) % 2
        return low + 2 * mid + 4 * ((z // 4 + j // 4) % 2)

    def z_peer(j):
        return place(x, other_z(j), h, yk)

    def yk_peer(j):
        return place(x, z, h, (yk + j) % YK)

    def y_peer(j):
        return place(x, z, h, ((y + j) % NY) * NK + k)

    core_peer = place(x, z, h, y * NK + (1 - k))
    h_peer = place(x, z, 1 - h, yk)

    def send(src, dst, ss, rs, dev):
        return pltpu.make_async_remote_copy(
            src_ref=src, dst_ref=dst, send_sem=ss, recv_sem=rs, device_id=dev, device_id_type=MESH_ID
        )

    def each(n, step, first=1):
        def run(j, carry):
            step(j)
            return carry

        lax.fori_loop(first, n, run, 0)

    def unrolled(n, step, first=1):
        for j in range(first, n):
            step(j)

    def launch(name, n, copy, first=1):
        unrolled(n, lambda j: copy(j).start(), first)
        pending.append(lambda: each(n, lambda j: copy(j).wait_send(), first))
        owed[name] = lambda: unrolled(n, lambda j: copy(j).wait_recv(), first)

    def arrive(name):
        owed.pop(name)()

    def finish():
        for name in list(owed):
            arrive(name)
        for wait in pending:
            wait()

    def aligned(start, size):
        return pl.ds(pl.multiple_of(start, size), size)

    def load(i):
        return pltpu.make_async_copy(
            cholesky.at[:, aligned(i * M, M)], slab.at[aligned(i * OWN, OWN)], sem_l.at[i]
        )

    first_loads = [
        pltpu.make_async_copy(trial.at[aligned(r * BLOCK, BLOCK)], own_t, sem_i.at[0]),
        pltpu.make_async_copy(walkers.at[yk], own_w.at[0], sem_i.at[1]),
        pltpu.make_async_copy(walkers.at[YK + yk], own_w.at[1], sem_i.at[2]),
    ]
    later_loads = [
        pltpu.make_async_copy(trial, tri, sem_i.at[3]),
        pltpu.make_async_copy(noise, noi, sem_i.at[4]),
        pltpu.make_async_copy(walkers.at[c], wz.at[z], sem_i.at[5]),
    ]
    for copy in first_loads:
        copy.start()

    barrier = pltpu.get_barrier_semaphore()

    def greet(dev):
        pl.semaphore_signal(barrier, inc=1, device_id=dev, device_id_type=MESH_ID)

    around = NX * 9

    def greet_near(e):
        at = e // NX
        at = (ring + (1 - 2 * (at % 2)) * (4 - at // 2) + 2 * NZ) % (2 * NZ)
        greet(place((x + (e + 1) % NX) % NX, at % NZ, at // NZ, yk))

    unrolled(around - 1, greet_near, 0)
    unrolled(YK, lambda j: greet(yk_peer(j)), 1)

    for copy in first_loads:
        copy.wait()
    for s in range(NH):
        cpart[s * NE : (s + 1) * NE, :] = exact(own_t[...], own_w[s], TN)

    each(BLOCK, lambda i: load(i).start(), 0)
    for copy in later_loads:
        copy.start()
    pl.semaphore_wait(barrier, around - 1 + YK - 1)

    def c_copy(e):
        at = near_z(e) % NZ + NZ * near_x(e)
        return send(cpart.at[aligned(8 * at, 8)], crs.at[e], s_c.at[e], r_c.at[e], near_peer(e))

    launch("c", ROWS - 1, c_copy, 0)

    each(BLOCK, lambda i: load(i).wait(), 0)
    for copy in later_loads:
        copy.wait()
    trial_split = split(tri[...])

    def prepare(b):
        rows = aligned(b * 128, 128)
        block = slab[rows, :]
        top, low = split(block)
        lt[yk, rows, :] = dot3((top, low), trial_split, NN)
        slab_top[rows, :] = top
        slab_low[rows, :] = low

    each(4, prepare, 0)
    launch("g", NY, lambda j: send(lt.at[yk], lt.at[yk], s_g.at[j], r_g.at[j], y_peer(j)))

    def g_copy(j):
        ref = lt.at[(y + j) % NY * NK + k]
        return send(ref, ref, s_h.at[j], r_h.at[j], core_peer)

    launch("h0", 1, g_copy, 0)

    crs[ROWS - 1] = cpart[aligned(8 * r, 8), :]
    arrive("c")
    cag[r] = jnp.sum(crs[...], axis=0)
    launch("a", ROWS - 1, lambda e: send(cag.at[r], cag.at[r], s_a.at[e], r_a.at[e], near_peer(e)), 0)

    def w_copy(at):
        return send(wz.at[at], wz.at[at], s_w.at[0], r_w.at[at], place(x, goal, h, yk))

    @pl.when(jnp.logical_not(at_goal))
    def _():
        w_copy(z).start()

    full_sub, full_lane = sub((128, 128)), lane((128, 128))
    pick_w = (sub((128, W)) // 8 == lane((128, W))).astype(F32)
    pick_g = (lane((OWN, 128)) % OWN == sub((OWN, 128))).astype(F32)
    noise_wide = exact(exact(pick_w, noi[...], NN), pick_g, NN)
    own_g = (sub((128, 128)) // OWN == yk) & (sub((128, 128)) % OWN == lane((128, 128)) % OWN)
    own_g = own_g.astype(F32)
    same_g = (sub((128, 128)) % OWN == lane((128, 128)) % OWN).astype(F32)
    one_lane = (lane((8, 128)) < OWN).astype(F32)

    arrive("a")

    def t_copy(n, q):
        def copy(j):
            ref = tbuf.at[n, x, pl.ds(q * (NE // CHAINS), NE // CHAINS)]
            return send(ref, ref, s_t.at[n, j, q], r_t.at[n, j, q], x_peer(j))

        return copy

    @pl.when(at_goal)
    def _():
        each(NZ, lambda j: w_copy((z + j) % NZ).wait_recv())
        tbuf[0, x] = jnp.transpose(wz[...].reshape(NZ * BLOCK, NE))
        for q in range(CHAINS):
            each(NX, lambda j, q=q: t_copy(0, q)(j).start())

    both = cag[...].reshape(NH * NE, NE)
    corr = [both[s * NE : (s + 1) * NE] for s in range(NH)]
    grams = tuple(exact(m, m, TN) for m in corr)

    def half_inverse(i, mats):
        @pl.when(i == 1)
        def _():
            arrive("g")
            launch("h", NY, g_copy)

        return eliminate(mats)

    inverses = lax.fori_loop(0, NE // 64, half_inverse, grams)
    for s in range(NH):
        left = exact(own_w[s], inverses[s], NN)
        own_v[s * BLOCK : (s + 1) * BLOCK] = exact(left, corr[s], NT)
    arrive("h0")
    arrive("h")
    held_v = split(own_v[...])
    shares = []
    row_lane = lane((NH * BLOCK, 512)) // OWN == sub((NH * BLOCK, 512)) % BLOCK
    for q in range(YK):
        cross = jnp.where(row_lane, dot3(held_v, split(lt[q]), NT), 0.0)
        cross = (cross[:, 0:128] + cross[:, 128:256]) + (cross[:, 256:384] + cross[:, 384:512])
        shares.append([jnp.sum(cross[s * BLOCK : (s + 1) * BLOCK], axis=0, keepdims=True) for s in range(NH)])
    shares = jnp.concatenate([shares[q][s] for s in range(NH) for q in range(YK)], axis=0)
    shares = exact(shares, same_g, NN)
    shares = jnp.where(lane((W, 128)) // OWN == sub((W, 128)) % YK, shares, 0.0)
    brs[r] = jnp.concatenate([jnp.sum(shares[8 * a : 8 * a + 8], axis=0, keepdims=True) for a in range(2)], axis=0)
    launch("b", ROWS - 1, lambda e: send(brs.at[r], brs.at[r], s_b.at[e], r_b.at[e], row_peer(e)), 0)
    arrive("b")
    ball[yk] = 0.1 * jnp.sum(brs[...], axis=0)
    launch("v", YK, lambda j: send(ball.at[yk], ball.at[yk], s_v.at[j], r_v.at[j], yk_peer(j)))
    arrive("v")

    bias_rows = [jnp.broadcast_to(ball[q, s : s + 1], (8, 128)) for s in range(NH) for q in range(YK)]
    bias_wide = exact(jnp.concatenate(bias_rows, axis=0), own_g, NN)
    field_full = noise_wide - bias_wide
    field_wide = jnp.where(full_sub % 8 == full_lane // OWN, 0.1 * field_full, 0.0)
    field_split = split(field_wide)

    def number(half, at_y, core):
        return half * YK + at_y * NK + core

    def piece(ref, lead, p):
        return ref.at[(*lead, pl.ds(8 * p, 8))]

    def k_copy(half, p):
        def copy(j):
            src = piece(pot, (number(half, (y + j) % NY, 1 - k),), p)
            return send(src, piece(rc, (half, j), p), s_k.at[half, j, p], r_k.at[half, j, p], core_peer)

        return copy

    def y_copy(half, p):
        def copy(j):
            src = piece(pot, (number(half, (y + j) % NY, k),), p)
            return send(src, piece(ry, (half, j), p), s_y.at[half, j, p], r_y.at[half, j, p], y_peer(j))

        return copy

    def add_core(half, p, j):
        k_copy(half, p)(j).wait_recv()
        mine = number(half, (y + j) % NY, k)
        at = pl.ds(8 * p, 8)
        pot[mine, at] = pot[mine, at] + rc[half, j, at]

    def start_y(half, p):
        def pass_on(j):
            add_core(half, p, j)
            y_copy(half, p)(j).start()

        unrolled(NY, pass_on, 1)
        pending.append(lambda: each(NY, lambda j: y_copy(half, p)(j).wait_send()))

    def end_y(half, p):
        add_core(half, p, 0)
        unrolled(NY, lambda j: y_copy(half, p)(j).wait_recv(), 1)
        mine = number(half, y, k)
        at = pl.ds(8 * p, 8)
        pot[mine, at] = (pot[mine, at] + ry[half, 1, at]) + (ry[half, 2, at] + ry[half, 3, at])

    def z_copy(half, p):
        src = piece(pot, (number(half, y, k),), p)
        return send(src, piece(pz, (ring,), p), s_z.at[half, p], r_z.at[ring, p], place(x, goal, half, yk))

    units = [(far, p) for p in range(PARTS) for far in (1, 0)]
    side = (h, 1 - h)
    for p in range(PARTS):
        rows = slice(p * 128, (p + 1) * 128)
        part = dot3(field_split, (slab_top[rows, :], slab_low[rows, :]), NN)
        pot[:, p * 8 : (p + 1) * 8, :] = part.reshape(W, 8, M)
        for half in (1 - h, h):
            unrolled(NY, lambda j, half=half, p=p: k_copy(half, p)(j).start(), 0)
        if p:
            for unit in units[2 * p - 2 : min(2 * p, AHEAD)]:
                start_y(side[unit[0]], unit[1])
    for half in (1 - h, h):
        for p in range(PARTS):
            pending.append(lambda half=half, p=p: each(NY, lambda j: k_copy(half, p)(j).wait_send(), 0))


    exponent = field_full * bias_wide - 0.5 * bias_wide * bias_wide
    lws[yk] = exact(one_lane, exponent, NT)[0:1]
    launch("l", YK, lambda j: send(lws.at[yk], lws.at[yk], s_l.at[j], r_l.at[j], yk_peer(j)))

    for at_unit, (far, p) in enumerate(units):
        half = side[far]
        end_y(half, p)
        if far:
            z_copy(half, p).start()
        else:

            @pl.when(jnp.logical_not(at_goal))
            def _(half=half, p=p):
                z_copy(half, p).start()

        if at_unit + AHEAD < len(units):
            unit = units[at_unit + AHEAD]
            start_y(side[unit[0]], unit[1])

    arrive("l")
    lwz[h] = jnp.sum(lws[...], axis=0)
    launch("m", 1, lambda j: send(lwz.at[h], lwz.at[h], s_m.at[0], r_m.at[0], h_peer), 0)

    arrive("m")
    total = lwz[0] + lwz[1]
    fold = lane((W, 128)) == 8 * sub((W, 128))
    weight[...] = exact(jnp.broadcast_to(total, (8, 128)), fold.astype(F32), NT)[0:1]

    @pl.when(at_goal)
    def _():
        pz[ring] = pot[number(h, y, k)]

        def came(source, p):
            ref = piece(pz, (source,), p)
            send(ref, ref, s_z.at[0, p], r_z.at[source, p], h_peer).wait_recv()

        def assemble(j):
            row = (z + j) % NZ

            @pl.when(j > 0)
            def _():
                each(PARTS, lambda p: came(h * NZ + row, p), 0)

            each(PARTS, lambda p: came((1 - h) * NZ + row, p), 0)
            top, low = split(pz[row] + pz[NZ + row])
            rows = aligned(row * BLOCK, BLOCK)
            for q in range(NX):
                ptop[q, rows] = top[:, q * NZ * BLOCK : (q + 1) * NZ * BLOCK]
                plow[q, rows] = low[:, q * NZ * BLOCK : (q + 1) * NZ * BLOCK]

        each(NZ, assemble, 0)
        span = [slice(q * (NE // CHAINS), (q + 1) * (NE // CHAINS)) for q in range(CHAINS)]
        sums = [tbuf[0, x, span[q]] for q in range(CHAINS)]
        for n in range(1, TAYLOR + 1):
            for q in range(CHAINS):
                term = jnp.zeros((NE // CHAINS, NZ * BLOCK), F32)
                for j in (0, 1, 3, 2):
                    if j:
                        t_copy(n - 1, q)(j).wait_recv()
                    at = (x + NX - j) % NX
                    term = term + dot3(split(tbuf[n - 1, at, span[q]]), (ptop[at], plow[at]), NT)
                term = term / float(n)
                sums[q] = sums[q] + term
                if n < TAYLOR:
                    tbuf[n, x, span[q]] = term
                    for j in (2, 1, 3):
                        t_copy(n, q)(j).start()
        sum_t = jnp.concatenate(sums, axis=0)
        fin[...] = jnp.transpose(sum_t).reshape(NZ, BLOCK, NE)

        def f_copy(j):
            return send(fin.at[(z + j) % NZ], got, s_f.at[j], r_f.at[0], place(x, (z + j) % NZ, h, yk))

        each(NZ, lambda j: f_copy(j).start())
        out[0] = fin[z]
        for n in range(TAYLOR):
            for q in range(CHAINS):
                each(NX, lambda j, n=n, q=q: t_copy(n, q)(j).wait_send())
        each(NZ, lambda j: f_copy(j).wait_send())

    @pl.when(jnp.logical_not(at_goal))
    def _():
        send(fin.at[0], got, s_f.at[0], r_f.at[0], h_peer).wait_recv()
        out[0] = got[...]

    for p in range(PARTS):
        z_copy(1 - h, p).wait_send()

    @pl.when(jnp.logical_not(at_goal))
    def _():
        w_copy(z).wait_send()
        for p in range(PARTS):
            z_copy(h, p).wait_send()

    finish()


def hand_over(propagated, weight, propagated_out, weight_out, sems):
    copies = [
        pltpu.make_async_copy(propagated, propagated_out, sems.at[0]),
        pltpu.make_async_copy(weight.at[0], weight_out, sems.at[1]),
    ]
    for copy in copies:
        copy.start()
    for copy in copies:
        copy.wait()


def call(walkers, trial, cholesky, noise, name="step", cid=0):
    vmem = pl.BlockSpec(memory_space=pltpu.VMEM)
    anywhere = pl.BlockSpec(memory_space=pltpu.HBM)
    dma = pltpu.SemaphoreType.DMA

    def pair(*shape):
        return [dma(shape), dma(shape)]

    propagated, weight = pl.pallas_call(
        kernel,
        name=name,
        out_shape=(jax.ShapeDtypeStruct((1, BLOCK, NE), F32), jax.ShapeDtypeStruct((1, W), F32)),
        in_specs=[anywhere] * 4,
        out_specs=(vmem, vmem),
        scratch_shapes=[
            pltpu.VMEM((NH, BLOCK, NE), F32),
            pltpu.VMEM((BLOCK, NE), F32),
            pltpu.VMEM((M, NE), F32),
            pltpu.VMEM((W, OWN), F32),
            pltpu.VMEM((512, M), F32),
            pltpu.VMEM((512, M), BF16),
            pltpu.VMEM((512, M), BF16),
            pltpu.VMEM((YK, 512, NE), F32),
            pltpu.VMEM((NH * NE, NE), F32),
            pltpu.VMEM((ROWS, 8, NE), F32),
            pltpu.VMEM((ROWS, 8, NE), F32),
            pltpu.VMEM((NZ, BLOCK, NE), F32),
            pltpu.VMEM((TAYLOR, NX, NE, NZ * BLOCK), F32),
            pltpu.VMEM((NH * BLOCK, NE), F32),
            pltpu.VMEM((YK, NH, 128), F32),
            pltpu.VMEM((ROWS, 2, 128), F32),
            pltpu.VMEM((W, BLOCK, M), F32),
            pltpu.VMEM((NH, NY, BLOCK, M), F32),
            pltpu.VMEM((NH, NY, BLOCK, M), F32),
            pltpu.VMEM((NH * NZ, BLOCK, M), F32),
            pltpu.VMEM((NX, NZ * BLOCK, NZ * BLOCK), BF16),
            pltpu.VMEM((NX, NZ * BLOCK, NZ * BLOCK), BF16),
            pltpu.VMEM((NZ, BLOCK, NE), F32),
            pltpu.VMEM((BLOCK, NE), F32),
            pltpu.VMEM((YK, 1, 128), F32),
            pltpu.VMEM((NH, 1, 128), F32),
            dma((BLOCK,)),
            dma((6,)),
            *pair(ROWS),
            *pair(ROWS),
            dma((1,)),
            dma((NZ,)),
            *pair(TAYLOR, NX, CHAINS),
            *pair(NY),
            *pair(NY),
            *pair(YK),
            *pair(ROWS),
            *pair(NH, NY, PARTS),
            *pair(NH, NY, PARTS),
            dma((NH, PARTS)),
            dma((NH * NZ, PARTS)),
            dma((NZ,)),
            dma((1,)),
            *pair(YK),
            *pair(1),
        ],
        compiler_params=pltpu.CompilerParams(collective_id=cid, has_side_effects=True, vmem_limit_bytes=215 * 2**18),
    )(walkers, trial, cholesky, noise)
    return pl.pallas_call(
        hand_over,
        name="hand_over",
        out_shape=(jax.ShapeDtypeStruct((1, BLOCK, NE), F32), jax.ShapeDtypeStruct((W,), F32)),
        in_specs=[pl.BlockSpec(memory_space=pl.ANY)] * 2,
        out_specs=(pl.BlockSpec(memory_space=pl.ANY), pl.BlockSpec(memory_space=pl.ANY)),
        scratch_shapes=[dma((2,))],
        compiler_params=pltpu.CompilerParams(vmem_limit_bytes=2**20),
    )(propagated, weight)


def body(walkers, trial, cholesky, noise):
    return call(walkers, trial, cholesky, noise)


def solution(mesh):
    return jax.shard_map(
        body,
        mesh=mesh,
        in_specs=(P(None, "rows", None), P(), P("chol", "rows"), P(None, "chol")),
        out_specs=(P("chol", "rows", None), P()),
        check_vma=False,
    )
```

```python
import jax
import jax.numpy as jnp
from jax import lax
from jax.experimental import pallas as pl
from jax.experimental.pallas import tpu as pltpu
from jax.sharding import PartitionSpec as P

M = 1024
NE = 128
TAYLOR = 6
NX, NZ, NH, NY, NK = 4, 8, 2, 4, 2
ROWS = NX * NZ
YK = NY * NK
BLOCK = M // ROWS
PARTS = BLOCK // 8
W = 16
OWN = 16
F32 = jnp.float32
BF16 = jnp.bfloat16
MESH_ID = pl.DeviceIdType.MESH
NT = (((1,), (1,)), ((), ()))
NN = (((1,), (0,)), ((), ()))
TN = (((0,), (0,)), ((), ()))
AHEAD = 3
CHAINS = 4


def exact(a, b, dims):
    return lax.dot_general(a, b, dims, precision=lax.Precision.HIGHEST, preferred_element_type=F32)


def split(a):
    top = a.astype(BF16)
    return top, (a - top.astype(F32)).astype(BF16)


def dot3(a, b, dims):
    def one(p, q):
        return lax.dot_general(p, q, dims, preferred_element_type=F32)

    rows = a[0].shape[0]
    both = one(jnp.concatenate(a, axis=0), b[0])
    return both[:rows] + (one(a[0], b[1]) + both[rows:])


def sub(index):
    return lax.broadcasted_iota(jnp.int32, index, 0)


def lane(index):
    return lax.broadcasted_iota(jnp.int32, index, 1)


def pivot_block(mat, base):
    row8, lane8, lanes = sub((8, NE)), lane((8, NE)), lane((NE, NE))

    def spread(rows):
        return [jnp.broadcast_to(rows[:, base + u : base + u + 1], (8, NE)) for u in range(8)]

    here, after = mat[base : base + 8], mat[base + 8 : base + 16]
    small, ahead = spread(here), spread(after)
    inside = (lane8 >= base) & (lane8 < base + 8)
    top = jnp.where(inside, (lane8 - base == row8).astype(F32), here)
    for t in range(8):
        inverse = 1.0 / jnp.broadcast_to(small[t][t : t + 1], (8, NE))
        pivot = small[t]
        for u in range(t + 1, 8):
            scaled = jnp.broadcast_to(small[u][t : t + 1], (8, NE)) * inverse
            small[u] = jnp.where(row8 == t, scaled, small[u] - pivot * scaled)
        scaled = jnp.broadcast_to(top[t : t + 1], (8, NE)) * inverse
        top = jnp.where(row8 == t, scaled, top - pivot * scaled)
    kept = jnp.where((lanes >= base) & (lanes < base + 8), 0.0, mat)
    rest = kept - exact(mat[:, base : base + 8], top, NN)
    part = [ahead[u] * top[u : u + 1] for u in range(8)]
    after = kept[base + 8 : base + 16] - (
        ((part[0] + part[1]) + (part[2] + part[3])) + ((part[4] + part[5]) + (part[6] + part[7]))
    )
    above = [rest[:base]] if base else []
    return jnp.concatenate([*above, top, after, rest[base + 16 :]], axis=0)


def eliminate(mats):
    for q in range(8):
        mats = [pivot_block(mat, 8 * q) for mat in mats]
    return tuple(pltpu.roll(jnp.concatenate([m[64:], m[:64]], axis=0), NE - 64, 1) for m in mats)


def kernel(
    walkers, trial, cholesky, noise, out, weight,
    own_w, own_t, tri, noi, slab, slab_top, slab_low, lt, cpart, crs, cag, wz, tbuf, own_v, ball, brs, pot, rc, ry, pz, ptop, plow, fin, got, lws, lwz,
    sem_l, sem_i, s_c, r_c, s_a, r_a, s_w, r_w, s_t, r_t, s_g, r_g, s_h, r_h, s_v, r_v, s_b, r_b, s_k, r_k, s_y, r_y, s_z, r_z, s_f, r_f, s_l, r_l, s_m, r_m,
):
    r = lax.axis_index("rows")
    c = lax.axis_index("chol")
    x, z = r // NZ, r % NZ
    h, yk = c // YK, c % YK
    y, k = yk // NK, yk % NK
    ring = h * NZ + z
    goal = 2 + 4 * k
    at_goal = z == goal
    pending = []
    owed = {}

    def place(at_x, at_z, at_h, at_yk):
        return (at_x * NZ + at_z, at_h * YK + at_yk)

    def row_peer(e):
        return place((x + (e + 1) % NX) % NX, other_z(NZ - 1 - e // NX), h, yk)

    def near_z(e):
        at = e // NX
        return (ring + (1 - at % 2) * (4 - at // 2) + (at % 2) * (at // 2 - 3) + 2 * NZ) % (2 * NZ)

    def near_x(e):
        return (x + (e + 1) % NX) % NX

    def near_peer(e):
        return place(near_x(e), near_z(e) % NZ, near_z(e) // NZ, yk)

    def x_peer(j):
        return place((x + j) % NX, z, h, yk)

    def other_z(j):
        low = (z % 2 + j % 2) % 2
        mid = (z // 2 % 2 + j // 2 % 2) % 2
        return low + 2 * mid + 4 * ((z // 4 + j // 4) % 2)

    def z_peer(j):
        return place(x, other_z(j), h, yk)

    def yk_peer(j):
        return place(x, z, h, (yk + j) % YK)

    def y_peer(j):
        return place(x, z, h, ((y + j) % NY) * NK + k)

    core_peer = place(x, z, h, y * NK + (1 - k))
    h_peer = place(x, z, 1 - h, yk)

    def send(src, dst, ss, rs, dev):
        return pltpu.make_async_remote_copy(
            src_ref=src, dst_ref=dst, send_sem=ss, recv_sem=rs, device_id=dev, device_id_type=MESH_ID
        )

    def each(n, step, first=1):
        def run(j, carry):
            step(j)
            return carry

        lax.fori_loop(first, n, run, 0)

    def unrolled(n, step, first=1):
        for j in range(first, n):
            step(j)

    def launch(name, n, copy, first=1):
        unrolled(n, lambda j: copy(j).start(), first)
        pending.append(lambda: each(n, lambda j: copy(j).wait_send(), first))
        owed[name] = lambda: unrolled(n, lambda j: copy(j).wait_recv(), first)

    def arrive(name):
        owed.pop(name)()

    def finish():
        for name in list(owed):
            arrive(name)
        for wait in pending:
            wait()

    def aligned(start, size):
        return pl.ds(pl.multiple_of(start, size), size)

    def load(i):
        return pltpu.make_async_copy(
            cholesky.at[:, aligned(i * M, M)], slab.at[aligned(i * OWN, OWN)], sem_l.at[i]
        )

    first_loads = [
        pltpu.make_async_copy(trial.at[aligned(r * BLOCK, BLOCK)], own_t, sem_i.at[0]),
        pltpu.make_async_copy(walkers.at[yk], own_w.at[0], sem_i.at[1]),
        pltpu.make_async_copy(walkers.at[YK + yk], own_w.at[1], sem_i.at[2]),
    ]
    later_loads = [
        pltpu.make_async_copy(trial, tri, sem_i.at[3]),
        pltpu.make_async_copy(noise, noi, sem_i.at[4]),
        pltpu.make_async_copy(walkers.at[c], wz.at[z], sem_i.at[5]),
    ]
    for copy in first_loads:
        copy.start()

    barrier = pltpu.get_barrier_semaphore()

    def greet(dev):
        pl.semaphore_signal(barrier, inc=1, device_id=dev, device_id_type=MESH_ID)

    around = NX * 9

    def greet_near(e):
        at = e // NX
        at = (ring + (1 - 2 * (at % 2)) * (4 - at // 2) + 2 * NZ) % (2 * NZ)
        greet(place((x + (e + 1) % NX) % NX, at % NZ, at // NZ, yk))

    unrolled(around - 1, greet_near, 0)
    unrolled(YK, lambda j: greet(yk_peer(j)), 1)

    for copy in first_loads:
        copy.wait()
    for s in range(NH):
        cpart[s * NE : (s + 1) * NE, :] = exact(own_t[...], own_w[s], TN)

    each(BLOCK, lambda i: load(i).start(), 0)
    for copy in later_loads:
        copy.start()
    pl.semaphore_wait(barrier, around - 1 + YK - 1)

    def c_copy(e):
        at = near_z(e) % NZ + NZ * near_x(e)
        return send(cpart.at[aligned(8 * at, 8)], crs.at[e], s_c.at[e], r_c.at[e], near_peer(e))

    launch("c", ROWS - 1, c_copy, 0)

    each(BLOCK, lambda i: load(i).wait(), 0)
    for copy in later_loads:
        copy.wait()
    trial_split = split(tri[...])

    def prepare(b):
        rows = aligned(b * 128, 128)
        block = slab[rows, :]
        top, low = split(block)
        lt[yk, rows, :] = dot3((top, low), trial_split, NN)
        slab_top[rows, :] = top
        slab_low[rows, :] = low

    each(4, prepare, 0)
    launch("g", NY, lambda j: send(lt.at[yk], lt.at[yk], s_g.at[j], r_g.at[j], y_peer(j)))

    def g_copy(j):
        ref = lt.at[(y + j) % NY * NK + k]
        return send(ref, ref, s_h.at[j], r_h.at[j], core_peer)

    launch("h0", 1, g_copy, 0)

    crs[ROWS - 1] = cpart[aligned(8 * r, 8), :]
    arrive("c")
    cag[r] = jnp.sum(crs[...], axis=0)
    launch("a", ROWS - 1, lambda e: send(cag.at[r], cag.at[r], s_a.at[e], r_a.at[e], near_peer(e)), 0)

    def w_copy(at):
        return send(wz.at[at], wz.at[at], s_w.at[0], r_w.at[at], place(x, goal, h, yk))

    @pl.when(jnp.logical_not(at_goal))
    def _():
        w_copy(z).start()

    full_sub, full_lane = sub((128, 128)), lane((128, 128))
    pick_w = (sub((128, W)) // 8 == lane((128, W))).astype(F32)
    pick_g = (lane((OWN, 128)) % OWN == sub((OWN, 128))).astype(F32)
    noise_wide = exact(exact(pick_w, noi[...], NN), pick_g, NN)
    own_g = (sub((128, 128)) // OWN == yk) & (sub((128, 128)) % OWN == lane((128, 128)) % OWN)
    own_g = own_g.astype(F32)
    same_g = (sub((128, 128)) % OWN == lane((128, 128)) % OWN).astype(F32)
    one_lane = (lane((8, 128)) < OWN).astype(F32)

    arrive("a")

    def t_copy(n, q):
        def copy(j):
            ref = tbuf.at[n, x, pl.ds(q * (NE // CHAINS), NE // CHAINS)]
            return send(ref, ref, s_t.at[n, j, q], r_t.at[n, j, q], x_peer(j))

        return copy

    @pl.when(at_goal)
    def _():
        each(NZ, lambda j: w_copy((z + j) % NZ).wait_recv())
        tbuf[0, x] = jnp.transpose(wz[...].reshape(NZ * BLOCK, NE))
        for q in range(CHAINS):
            each(NX, lambda j, q=q: t_copy(0, q)(j).start())

    both = cag[...].reshape(NH * NE, NE)
    corr = [both[s * NE : (s + 1) * NE] for s in range(NH)]
    grams = tuple(exact(m, m, TN) for m in corr)

    def half_inverse(i, mats):
        @pl.when(i == 1)
        def _():
            arrive("g")
            launch("h", NY, g_copy)

        return eliminate(mats)

    inverses = lax.fori_loop(0, NE // 64, half_inverse, grams)
    for s in range(NH):
        left = exact(own_w[s], inverses[s], NN)
        own_v[s * BLOCK : (s + 1) * BLOCK] = exact(left, corr[s], NT)
    arrive("h0")
    arrive("h")
    held_v = split(own_v[...])
    shares = []
    row_lane = lane((NH * BLOCK, 512)) // OWN == sub((NH * BLOCK, 512)) % BLOCK
    for q in range(YK):
        cross = jnp.where(row_lane, dot3(held_v, split(lt[q]), NT), 0.0)
        cross = (cross[:, 0:128] + cross[:, 128:256]) + (cross[:, 256:384] + cross[:, 384:512])
        shares.append([jnp.sum(cross[s * BLOCK : (s + 1) * BLOCK], axis=0, keepdims=True) for s in range(NH)])
    shares = jnp.concatenate([shares[q][s] for s in range(NH) for q in range(YK)], axis=0)
    shares = exact(shares, same_g, NN)
    shares = jnp.where(lane((W, 128)) // OWN == sub((W, 128)) % YK, shares, 0.0)
    brs[r] = jnp.concatenate([jnp.sum(shares[8 * a : 8 * a + 8], axis=0, keepdims=True) for a in range(2)], axis=0)
    launch("b", ROWS - 1, lambda e: send(brs.at[r], brs.at[r], s_b.at[e], r_b.at[e], row_peer(e)), 0)
    arrive("b")
    ball[yk] = 0.1 * jnp.sum(brs[...], axis=0)
    launch("v", YK, lambda j: send(ball.at[yk], ball.at[yk], s_v.at[j], r_v.at[j], yk_peer(j)))
    arrive("v")

    bias_rows = [jnp.broadcast_to(ball[q, s : s + 1], (8, 128)) for s in range(NH) for q in range(YK)]
    bias_wide = exact(jnp.concatenate(bias_rows, axis=0), own_g, NN)
    field_full = noise_wide - bias_wide
    field_wide = jnp.where(full_sub % 8 == full_lane // OWN, 0.1 * field_full, 0.0)
    field_split = split(field_wide)

    def number(half, at_y, core):
        return half * YK + at_y * NK + core

    def piece(ref, lead, p):
        return ref.at[(*lead, pl.ds(8 * p, 8))]

    def k_copy(half, p):
        def copy(j):
            src = piece(pot, (number(half, (y + j) % NY, 1 - k),), p)
            return send(src, piece(rc, (half, j), p), s_k.at[half, j, p], r_k.at[half, j, p], core_peer)

        return copy

    def y_copy(half, p):
        def copy(j):
            src = piece(pot, (number(half, (y + j) % NY, k),), p)
            return send(src, piece(ry, (half, j), p), s_y.at[half, j, p], r_y.at[half, j, p], y_peer(j))

        return copy

    def add_core(half, p, j):
        k_copy(half, p)(j).wait_recv()
        mine = number(half, (y + j) % NY, k)
        at = pl.ds(8 * p, 8)
        pot[mine, at] = pot[mine, at] + rc[half, j, at]

    def start_y(half, p):
        def pass_on(j):
            add_core(half, p, j)
            y_copy(half, p)(j).start()

        unrolled(NY, pass_on, 1)
        pending.append(lambda: each(NY, lambda j: y_copy(half, p)(j).wait_send()))

    def end_y(half, p):
        add_core(half, p, 0)
        unrolled(NY, lambda j: y_copy(half, p)(j).wait_recv(), 1)
        mine = number(half, y, k)
        at = pl.ds(8 * p, 8)
        pot[mine, at] = (pot[mine, at] + ry[half, 1, at]) + (ry[half, 2, at] + ry[half, 3, at])

    def z_copy(half, p):
        src = piece(pot, (number(half, y, k),), p)
        return send(src, piece(pz, (ring,), p), s_z.at[half, p], r_z.at[ring, p], place(x, goal, half, yk))

    units = [(far, p) for p in range(PARTS) for far in (1, 0)]
    side = (h, 1 - h)
    for p in range(PARTS):
        rows = slice(p * 128, (p + 1) * 128)
        part = dot3(field_split, (slab_top[rows, :], slab_low[rows, :]), NN)
        pot[:, p * 8 : (p + 1) * 8, :] = part.reshape(W, 8, M)
        for half in (1 - h, h):
            unrolled(NY, lambda j, half=half, p=p: k_copy(half, p)(j).start(), 0)
        if p:
            for unit in units[2 * p - 2 : min(2 * p, AHEAD)]:
                start_y(side[unit[0]], unit[1])
    for half in (1 - h, h):
        for p in range(PARTS):
            pending.append(lambda half=half, p=p: each(NY, lambda j: k_copy(half, p)(j).wait_send(), 0))


    exponent = field_full * bias_wide - 0.5 * bias_wide * bias_wide
    lws[yk] = exact(one_lane, exponent, NT)[0:1]
    launch("l", YK, lambda j: send(lws.at[yk], lws.at[yk], s_l.at[j], r_l.at[j], yk_peer(j)))

    for at_unit, (far, p) in enumerate(units):
        half = side[far]
        end_y(half, p)
        if far:
            z_copy(half, p).start()
        else:

            @pl.when(jnp.logical_not(at_goal))
            def _(half=half, p=p):
                z_copy(half, p).start()

        if at_unit + AHEAD < len(units):
            unit = units[at_unit + AHEAD]
            start_y(side[unit[0]], unit[1])

    arrive("l")
    lwz[h] = jnp.sum(lws[...], axis=0)
    launch("m", 1, lambda j: send(lwz.at[h], lwz.at[h], s_m.at[0], r_m.at[0], h_peer), 0)

    arrive("m")
    total = lwz[0] + lwz[1]
    fold = lane((W, 128)) == 8 * sub((W, 128))
    weight[...] = exact(jnp.broadcast_to(total, (8, 128)), fold.astype(F32), NT)[0:1]

    @pl.when(at_goal)
    def _():
        pz[ring] = pot[number(h, y, k)]

        def came(source, p):
            ref = piece(pz, (source,), p)
            send(ref, ref, s_z.at[0, p], r_z.at[source, p], h_peer).wait_recv()

        def assemble(j):
            row = (z + j) % NZ

            @pl.when(j > 0)
            def _():
                each(PARTS, lambda p: came(h * NZ + row, p), 0)

            each(PARTS, lambda p: came((1 - h) * NZ + row, p), 0)
            top, low = split(pz[row] + pz[NZ + row])
            rows = aligned(row * BLOCK, BLOCK)
            for q in range(NX):
                ptop[q, rows] = top[:, q * NZ * BLOCK : (q + 1) * NZ * BLOCK]
                plow[q, rows] = low[:, q * NZ * BLOCK : (q + 1) * NZ * BLOCK]

        each(NZ, assemble, 0)
        span = [slice(q * (NE // CHAINS), (q + 1) * (NE // CHAINS)) for q in range(CHAINS)]
        sums = [tbuf[0, x, span[q]] for q in range(CHAINS)]
        for n in range(1, TAYLOR + 1):
            own = dot3(split(tbuf[n - 1, x]), (ptop[x], plow[x]), NT)
            for q in range(CHAINS):
                term = own[span[q]]
                for j in (1, 3, 2):
                    t_copy(n - 1, q)(j).wait_recv()
                    at = (x + NX - j) % NX
                    term = term + dot3(split(tbuf[n - 1, at, span[q]]), (ptop[at], plow[at]), NT)
                term = term / float(n)
                sums[q] = sums[q] + term
                if n < TAYLOR:
                    tbuf[n, x, span[q]] = term
                    for j in (2, 1, 3):
                        t_copy(n, q)(j).start()
        sum_t = jnp.concatenate(sums, axis=0)
        fin[...] = jnp.transpose(sum_t).reshape(NZ, BLOCK, NE)

        def f_copy(j):
            return send(fin.at[(z + j) % NZ], got, s_f.at[j], r_f.at[0], place(x, (z + j) % NZ, h, yk))

        each(NZ, lambda j: f_copy(j).start())
        out[0] = fin[z]
        for n in range(TAYLOR):
            for q in range(CHAINS):
                each(NX, lambda j, n=n, q=q: t_copy(n, q)(j).wait_send())
        each(NZ, lambda j: f_copy(j).wait_send())

    @pl.when(jnp.logical_not(at_goal))
    def _():
        send(fin.at[0], got, s_f.at[0], r_f.at[0], h_peer).wait_recv()
        out[0] = got[...]

    for p in range(PARTS):
        z_copy(1 - h, p).wait_send()

    @pl.when(jnp.logical_not(at_goal))
    def _():
        w_copy(z).wait_send()
        for p in range(PARTS):
            z_copy(h, p).wait_send()

    finish()


def hand_over(propagated, weight, propagated_out, weight_out, sems):
    copies = [
        pltpu.make_async_copy(propagated, propagated_out, sems.at[0]),
        pltpu.make_async_copy(weight.at[0], weight_out, sems.at[1]),
    ]
    for copy in copies:
        copy.start()
    for copy in copies:
        copy.wait()


def call(walkers, trial, cholesky, noise, name="step", cid=0):
    vmem = pl.BlockSpec(memory_space=pltpu.VMEM)
    anywhere = pl.BlockSpec(memory_space=pltpu.HBM)
    dma = pltpu.SemaphoreType.DMA

    def pair(*shape):
        return [dma(shape), dma(shape)]

    propagated, weight = pl.pallas_call(
        kernel,
        name=name,
        out_shape=(jax.ShapeDtypeStruct((1, BLOCK, NE), F32), jax.ShapeDtypeStruct((1, W), F32)),
        in_specs=[anywhere] * 4,
        out_specs=(vmem, vmem),
        scratch_shapes=[
            pltpu.VMEM((NH, BLOCK, NE), F32),
            pltpu.VMEM((BLOCK, NE), F32),
            pltpu.VMEM((M, NE), F32),
            pltpu.VMEM((W, OWN), F32),
            pltpu.VMEM((512, M), F32),
            pltpu.VMEM((512, M), BF16),
            pltpu.VMEM((512, M), BF16),
            pltpu.VMEM((YK, 512, NE), F32),
            pltpu.VMEM((NH * NE, NE), F32),
            pltpu.VMEM((ROWS, 8, NE), F32),
            pltpu.VMEM((ROWS, 8, NE), F32),
            pltpu.VMEM((NZ, BLOCK, NE), F32),
            pltpu.VMEM((TAYLOR, NX, NE, NZ * BLOCK), F32),
            pltpu.VMEM((NH * BLOCK, NE), F32),
            pltpu.VMEM((YK, NH, 128), F32),
            pltpu.VMEM((ROWS, 2, 128), F32),
            pltpu.VMEM((W, BLOCK, M), F32),
            pltpu.VMEM((NH, NY, BLOCK, M), F32),
            pltpu.VMEM((NH, NY, BLOCK, M), F32),
            pltpu.VMEM((NH * NZ, BLOCK, M), F32),
            pltpu.VMEM((NX, NZ * BLOCK, NZ * BLOCK), BF16),
            pltpu.VMEM((NX, NZ * BLOCK, NZ * BLOCK), BF16),
            pltpu.VMEM((NZ, BLOCK, NE), F32),
            pltpu.VMEM((BLOCK, NE), F32),
            pltpu.VMEM((YK, 1, 128), F32),
            pltpu.VMEM((NH, 1, 128), F32),
            dma((BLOCK,)),
            dma((6,)),
            *pair(ROWS),
            *pair(ROWS),
            dma((1,)),
            dma((NZ,)),
            *pair(TAYLOR, NX, CHAINS),
            *pair(NY),
            *pair(NY),
            *pair(YK),
            *pair(ROWS),
            *pair(NH, NY, PARTS),
            *pair(NH, NY, PARTS),
            dma((NH, PARTS)),
            dma((NH * NZ, PARTS)),
            dma((NZ,)),
            dma((1,)),
            *pair(YK),
            *pair(1),
        ],
        compiler_params=pltpu.CompilerParams(collective_id=cid, has_side_effects=True, vmem_limit_bytes=215 * 2**18),
    )(walkers, trial, cholesky, noise)
    return pl.pallas_call(
        hand_over,
        name="hand_over",
        out_shape=(jax.ShapeDtypeStruct((1, BLOCK, NE), F32), jax.ShapeDtypeStruct((W,), F32)),
        in_specs=[pl.BlockSpec(memory_space=pl.ANY)] * 2,
        out_specs=(pl.BlockSpec(memory_space=pl.ANY), pl.BlockSpec(memory_space=pl.ANY)),
        scratch_shapes=[dma((2,))],
        compiler_params=pltpu.CompilerParams(vmem_limit_bytes=2**20),
    )(propagated, weight)


def body(walkers, trial, cholesky, noise):
    return call(walkers, trial, cholesky, noise)


def solution(mesh):
    return jax.shard_map(
        body,
        mesh=mesh,
        in_specs=(P(None, "rows", None), P(), P("chol", "rows"), P(None, "chol")),
        out_specs=(P("chol", "rows", None), P()),
        check_vma=False,
    )
```
